32 devices in a mesh: group: 8 (over z, x), row: 4 (over y, core).
Axes of the slice: x: 2, y: 2, z: 4, core: 2. Of those that a mesh axis runs over, the one named last changes fastest.
Arguments:
- video_frames: bfloat16 [32, 16, 192, 128], P('group', 'row'), may hold values from -6 to 6
- pred_owner: int32 [8], P('group'), may hold values from -1 to 6, as said below
- frame_counts: int32 [8], P('group'), may hold values from 2 to 4, as said below
- norm1_gain: float32 [128], replicated, may hold values from 0.1 to 1.9
- conv1_weight: bfloat16 [3, 3, 3, 128, 128], replicated, may hold values from -0.109375 to 0.109375
- conv1_bias: float32 [128], replicated, may hold values from -3 to 3
- norm2_gain: float32 [128], replicated, may hold values from 0.1 to 1.9
- conv2_weight: bfloat16 [3, 3, 3, 128, 256], replicated, may hold values from -0.109375 to 0.109375
- conv2_bias: float32 [256], replicated, may hold values from -3 to 3
Outputs:
- encoded: bfloat16 [16, 8, 96, 256], P('group', 'row')
The draws below stay inside these ranges and needn't reach their ends.
Inputs may be any that keep to these rules, and one draw needn't show every extreme that they name: `pred_owner`: -1 marks a video's first group; otherwise it is the nearest earlier group of the same video, 1 to 4 groups earlier. No group is the predecessor of two groups. Group 0 has none. `frame_counts`: every count is even; a group that precedes another group holds 4 frames, only a video's last group may hold fewer.
All inputs are finite; a program needn't handle non-finite values.
Results may differ from the reference program's by a relative error of at most 0.0046.
Values may be sent and summed in bfloat16 or wider, within the bound.
No kernel may reach another device: no remote copies, remote signals or barrier semaphores. Data moves between devices by JAX's collectives and lax.ppermute only.
A program may use at most 64 MiB of HBM per device.

```python
import jax
import jax.numpy as jnp
from jax import lax

C = 128
C2 = 256
FR = 4
W = 192
SPAN = 4
FRAMES = 32
H = 16
N_GROUP = 8


def chain_owners(key):
    positions = jnp.arange(N_GROUP, dtype=jnp.int32)
    stream_key, start_key = jax.random.split(jax.random.fold_in(key, 11))
    streams = jax.random.randint(stream_key, (N_GROUP,), 0, SPAN, dtype=jnp.int32)
    streams = jnp.where(positions < SPAN, positions, streams)
    streams = jnp.where(positions == SPAN, 0, streams)
    streams = jnp.where(positions == N_GROUP - 1, streams[N_GROUP - 2], streams)
    owners = jnp.full((N_GROUP,), -1, jnp.int32)
    for offset in reversed(range(1, SPAN + 1)):
        earlier = jnp.roll(streams, offset)
        match = (earlier == streams) & (positions >= offset)
        owners = jnp.where(match, positions - offset, owners)
    starts = jax.random.randint(start_key, (N_GROUP,), 0, 4, dtype=jnp.int32) == 0
    forced = (positions == SPAN) | (positions == N_GROUP - 1)
    return jnp.where(starts & ~forced, -1, owners).astype(jnp.int32)


def draw_pred_owner(key, part):
    return chain_owners(key)


def draw_frame_counts(key, part):
    positions = jnp.arange(N_GROUP, dtype=jnp.int32)
    owners = chain_owners(key)
    has_next = jnp.any(owners[None, :] == positions[:, None], axis=1)
    halves = jax.random.randint(jax.random.fold_in(key, 23), (N_GROUP,), 1, FR // 2 + 1, dtype=jnp.int32)
    halves = jnp.where(positions == N_GROUP - 1, 1, halves)
    return jnp.where(has_next, FR, 2 * halves).astype(jnp.int32)


def shard_levels(rng, dims, pieces, smallest, largest):
    gain, own = 1.0, jax.random.fold_in(rng, 6)
    for position, shards_of in pieces:
        steps = jnp.exp(jax.random.uniform(jax.random.fold_in(own, position), (shards_of,), jnp.float32, smallest / len(pieces), largest / len(pieces)))
        gain = gain * jnp.repeat(steps, dims[position] // shards_of).reshape([-1 if axis == position else 1 for axis in range(len(dims))])
    return gain


def normal_values(key, dims, scale, limit, shards=(), kind=jnp.bfloat16):
    drawn = jax.random.normal(key, dims, jnp.float32) * scale
    if len(shards) > 0:
        drawn = shard_levels(key, dims, shards, -0.22, 0.18) * drawn
    return jnp.clip(drawn, min=-limit, max=limit).astype(kind)


def setup_inputs(seed: int = 0) -> dict:
    splits = jax.random.split(jax.random.key(seed), 10)
    return {
        "video_frames": normal_values(splits[0], (FRAMES, H, W, C), 1.0, 6.0, ((0, 8), (1, 4))),
        "pred_owner": draw_pred_owner(jax.random.fold_in(splits[9], 71), 0),
        "frame_counts": draw_frame_counts(jax.random.fold_in(splits[9], 71), 0),
        "norm1_gain": jnp.clip(1.0 + 0.18 * jax.random.normal(splits[3], (C,), jnp.float32), 0.1, 1.9),
        "conv1_weight": normal_values(splits[4], (3, 3, 3, C, C), (27 * C) ** -0.5, 0.109375),
        "conv1_bias": normal_values(splits[5], (C,), 0.5, 3.0, (), jnp.float32),
        "norm2_gain": jnp.clip(1.0 + 0.18 * jax.random.normal(splits[6], (C,), jnp.float32), 0.1, 1.9),
        "conv2_weight": normal_values(splits[7], (3, 3, 3, C, C2), (27 * C) ** -0.5, 0.109375),
        "conv2_bias": normal_values(splits[8], (C2,), 0.5, 3.0, (), jnp.float32),
    }


def prepare(values, norm_gain):
    values = values.astype(jnp.float32)
    inverse = lax.rsqrt(lax.optimization_barrier(jnp.mean(values * values, axis=-1, keepdims=True)) + 1e-06)
    return jax.nn.silu(values * inverse * norm_gain).astype(jnp.bfloat16)

def conv_steady(padded, weight, out_frames, out_rows):
    channels = padded.shape[-1]
    columns = padded.shape[2] - 2
    outputs = weight.shape[-1]
    summed = jnp.zeros((out_frames * out_rows * columns, outputs), jnp.float32)
    for step_t in range(3):
        for step_h in range(3):
            window = jnp.concatenate([padded[step_t:step_t + out_frames, step_h:step_h + out_rows, step_w:step_w + columns] for step_w in range(3)], axis=-1)
            flattened = window.reshape(out_frames * out_rows * columns, 3 * channels)
            summed = summed + jnp.dot(flattened, weight[step_t, step_h].reshape(3 * channels, outputs), preferred_element_type=jnp.float32)
    return summed.reshape(out_frames, out_rows, columns, outputs)

def conv_stride(padded, weight, out_frames, out_rows):
    channels = padded.shape[-1]
    out_cols = (padded.shape[2] - 2) // 2
    outputs = weight.shape[-1]
    summed = jnp.zeros((out_frames * out_rows * out_cols, outputs), jnp.float32)
    for step_t in range(3):
        for step_h in range(3):
            window = jnp.concatenate([padded[step_t:step_t + 2 * out_frames:2, step_h:step_h + 2 * out_rows:2, step_w:step_w + 2 * out_cols:2] for step_w in range(3)], axis=-1)
            flattened = window.reshape(out_frames * out_rows * out_cols, 3 * channels)
            summed = summed + jnp.dot(flattened, weight[step_t, step_h].reshape(3 * channels, outputs), preferred_element_type=jnp.float32)
    return summed.reshape(out_frames, out_rows, out_cols, outputs)

def last_frames(clip, valid_count, amount):
    return lax.dynamic_slice_in_dim(clip, (valid_count - amount).astype(jnp.int32), amount, 0)

def reference(video_frames, pred_owner, frame_counts, norm1_gain, conv1_weight, conv1_bias, norm2_gain, conv2_weight, conv2_bias):
    groups = pred_owner.shape[0]
    rows = video_frames.shape[1]
    columns = video_frames.shape[2]
    channels = video_frames.shape[3]
    clips = video_frames.reshape(groups, FR, rows, columns, channels)
    source = jnp.maximum(pred_owner, 0).astype(jnp.int32)
    has_prior = (pred_owner >= 0)[:, None, None, None, None]
    hidden = prepare(clips, norm1_gain)
    tails_one = jax.vmap(lambda clip, valid_count: last_frames(clip, valid_count, 2))(hidden, frame_counts)
    before_one = jnp.where(has_prior, tails_one[source], jnp.zeros_like(tails_one))

    def layer_one(item):
        prior, clip, inputs = item
        extended = jnp.concatenate([prior, clip], 0)
        padded = jnp.pad(extended, ((0, 0), (1, 1), (1, 1), (0, 0)))
        mixed = conv_steady(padded, conv1_weight, FR, rows)
        return prepare(inputs.astype(jnp.float32) + mixed + conv1_bias, norm2_gain)
    second = lax.map(layer_one, (before_one, hidden, clips))
    tails_two = jax.vmap(lambda clip, valid_count: last_frames(clip, valid_count, 1))(second, frame_counts)
    before_two = jnp.where(has_prior, tails_two[source], jnp.zeros_like(tails_two))

    def layer_two(item):
        prior, clip, valid_count = item
        extended = jnp.concatenate([prior, clip], 0)
        padded = jnp.pad(extended, ((0, 0), (1, 0), (1, 1), (0, 0)))
        mixed = conv_stride(padded, conv2_weight, FR // 2, rows // 2) + conv2_bias
        keep = jnp.arange(FR // 2) < valid_count // 2
        return jnp.where(keep[:, None, None, None], mixed, 0.0).astype(jnp.bfloat16)
    encoded = lax.map(layer_two, (before_two, second, frame_counts))
    return encoded.reshape(groups * (FR // 2), rows // 2, columns // 2, conv2_weight.shape[-1])
```

```python
import functools

import jax
import jax.numpy as jnp
from jax import lax
from jax.experimental import pallas as pl
from jax.experimental.pallas import tpu as pltpu
from jax.sharding import PartitionSpec as P

ABOVE = 2
VMEM = pltpu.VMEM
SMEM = pltpu.SMEM
F32 = jnp.float32
BF16 = jnp.bfloat16


def shifted(value, axis, steps):
    count = lax.axis_size(axis)
    first, last = (max(0, -steps), min(count, count - steps))
    return lax.ppermute(value, axis, [(source, source + steps) for source in range(first, last)])


def swapped(value, axis, offset):
    count = lax.axis_size(axis)
    pairs = []
    for low in range(offset, count - 1, 2):
        pairs += [(low, low + 1), (low + 1, low)]
    return lax.ppermute(value, axis, pairs)


def pixel_silu(values, gain):
    inverse = lax.rsqrt(jnp.mean(values * values, axis=-1, keepdims=True) + 1e-06)
    half = values * inverse * (0.5 * gain)
    return half + half * jnp.tanh(half)


def column_window(row):
    width = row.shape[0]
    column = lax.broadcasted_iota(jnp.int32, row.shape, 0)
    left = jnp.where(column == 0, 0.0, pltpu.roll(row, 1, 0))
    right = jnp.where(column == width - 1, 0.0, pltpu.roll(row, width - 1, 0))
    return jnp.concatenate([left.astype(BF16), row.astype(BF16), right.astype(BF16)], axis=-1)


def fill_hidden(read, gain, window_ref, frame, rows):
    for row in range(rows):
        window_ref[frame, row] = column_window(pixel_silu(read(row), gain))


def conv1_rows(window_ref, frame, rows, weight):
    width, depth = window_ref.shape[2], window_ref.shape[3]
    total = None
    for tap in range(3):
        part = jnp.dot(
            window_ref[frame, tap : tap + rows].reshape(rows * width, depth),
            weight(tap),
            preferred_element_type=F32,
        )
        total = part if total is None else total + part
    return total


def fill_second(values, gain, first_row, stage_ref, strided_ref, slot):
    rows, half = strided_ref.shape[1], strided_ref.shape[2]
    width, channels = 2 * half, stage_ref.shape[2]
    for row in range(rows):
        ready = pixel_silu(values(row), gain).astype(BF16).astype(F32)
        if row == 0:
            ready = jnp.where(first_row, 0.0, ready)
        stage_ref[row, 0:8] = jnp.zeros((8, channels), F32)
        stage_ref[row, 8 : 8 + width] = ready
        strided_ref[slot, row] = jnp.concatenate(
            [stage_ref[row, pl.ds(7 + tap, half, stride=2), :].astype(BF16) for tap in range(3)],
            axis=-1,
        )


def conv2_frame(strided_ref, slot, weight_ref, step):
    total = None
    for tap in range(3):
        window = jnp.concatenate([strided_ref[slot, tap], strided_ref[slot, tap + 2]], axis=0)
        part = jnp.dot(window, weight_ref[step, tap], preferred_element_type=F32)
        total = part if total is None else total + part
    return total


def pick_rows(even, first, second):
    return jnp.where(even, first, second)


def row_reader(video_ref, frame, pair_ref, cross_ref, even):
    def read(row):
        if row < ABOVE:
            return jnp.where(even, cross_ref[frame, row].astype(F32), pair_ref[frame, row].astype(F32))
        if row < ABOVE + 4:
            return video_ref[frame, row - ABOVE].astype(F32)
        return jnp.where(even, pair_ref[frame, 0].astype(F32), cross_ref[frame, 0].astype(F32))

    return read


def send_kernel(
    flag_ref, video_ref, pair_ref, cross_ref, gain1_ref, weight1_ref, bias1_ref, gain2_ref,
    weight2_ref, prior_ref, tail_ref, strided_out_ref, window_ref, stage_ref, total_ref,
):
    even, first_row = flag_ref[0] == 1, flag_ref[1] == 1
    width = video_ref.shape[2]
    channels = video_ref.shape[3]
    readers = [row_reader(video_ref, f, pair_ref, cross_ref, even) for f in range(4)]
    for slot, frame in enumerate((1, 2, 3)):
        fill_hidden(readers[frame], gain1_ref[...], window_ref, slot, 7)
    both = conv1_rows(
        window_ref, 1, 5,
        lambda tap: jnp.concatenate([weight1_ref[1, tap], weight1_ref[0, tap]], axis=-1),
    )
    prior_ref[...] = both[:, channels:].astype(BF16).reshape(prior_ref.shape)
    total_ref[...] = (
        both[:, :channels]
        + conv1_rows(window_ref, 0, 5, lambda tap: weight1_ref[0, tap])
        + conv1_rows(window_ref, 2, 5, lambda tap: weight1_ref[2, tap])
    ).reshape(total_ref.shape)
    fill_second(
        lambda row: total_ref[row] + readers[3](row + 1) + bias1_ref[...],
        gain2_ref[...], first_row, stage_ref, strided_out_ref, 0,
    )
    tail_ref[...] = conv2_frame(strided_out_ref, 0, weight2_ref, 0).astype(BF16).reshape(tail_ref.shape)


def own_kernel(
    flag_ref, video_ref, pair_ref, cross_ref, gain1_ref, weight1_ref, bias1_ref, gain2_ref,
    weight2_ref, bias2_ref, strided3_ref, first_ref, next_ref, late_ref,
    window_ref, stage_ref, strided_ref, total_ref,
):
    even, first_row = flag_ref[0] == 1, flag_ref[1] == 1
    width = video_ref.shape[2]
    channels = video_ref.shape[3]
    readers = [row_reader(video_ref, f, pair_ref, cross_ref, even) for f in range(4)]
    for frame in range(3):
        fill_hidden(readers[frame], gain1_ref[...], window_ref, frame, 7)
    both = conv1_rows(
        window_ref, 0, 5,
        lambda tap: jnp.concatenate([weight1_ref[0, tap], weight1_ref[1, tap]], axis=-1),
    ) + conv1_rows(
        window_ref, 1, 5,
        lambda tap: jnp.concatenate([weight1_ref[1, tap], weight1_ref[2, tap]], axis=-1),
    )
    next_ref[...] = both[:, channels:].reshape(next_ref.shape)
    total_ref[...] = (
        both[:, :channels] + conv1_rows(window_ref, 2, 5, lambda tap: weight1_ref[2, tap])
    ).reshape(total_ref.shape)
    first_ref[...] = conv1_rows(window_ref, 0, 5, lambda tap: weight1_ref[2, tap]).reshape(first_ref.shape)
    for row in range(5):
        next_ref[row] += readers[1](row + 1) + bias1_ref[...]
        first_ref[row] += readers[0](row + 1) + bias1_ref[...]
    fill_second(
        lambda row: total_ref[row] + readers[2](row + 1) + bias1_ref[...],
        gain2_ref[...], first_row, stage_ref, strided_ref, 0,
    )
    late_ref[...] = (
        conv2_frame(strided_ref, 0, weight2_ref, 1)
        + conv2_frame(strided3_ref, 0, weight2_ref, 2)
        + bias2_ref[...]
    )


def next_kernel(
    flag_ref, prior_ref, pair_ref, cross_ref, gain1_ref, weight1_ref, gain2_ref,
    weight2_ref, bias2_ref, first_ref, next_ref, late_ref, second_out_ref, first_out_ref, early_ref,
    window_ref, stage_ref, strided_ref, total_ref,
):
    even, first_row, keep = flag_ref[0] == 1, flag_ref[1] == 1, flag_ref[2] == 1
    channels = prior_ref.shape[3]
    fill_hidden(
        row_reader(prior_ref, 0, pair_ref, cross_ref, even), gain1_ref[...], window_ref, 0, 7
    )
    both = conv1_rows(
        window_ref, 0, 5,
        lambda tap: jnp.concatenate([weight1_ref[0, tap], weight1_ref[1, tap]], axis=-1),
    )
    total_ref[...] = both[:, :channels].reshape(total_ref.shape)
    first_out_ref[...] = first_ref[...] + both[:, channels:].reshape(first_ref.shape)
    fill_second(
        lambda row: total_ref[row] + next_ref[row],
        gain2_ref[...], first_row, stage_ref, strided_ref, 0,
    )
    late = late_ref[...] + conv2_frame(strided_ref, 0, weight2_ref, 0)
    second_out_ref[...] = jnp.where(keep, late, 0.0).astype(BF16).reshape(second_out_ref.shape)
    early_ref[...] = conv2_frame(strided_ref, 0, weight2_ref, 2) + bias2_ref[...]


def last_kernel(
    flag_ref, prior_a_ref, prior_b_ref, prior_c_ref, tail_a_ref, tail_b_ref, tail_c_ref,
    gain2_ref, weight2_ref, first_ref, early_ref, done_ref, out_ref, stage_ref, strided_ref,
):
    first_row, distance = flag_ref[1] == 1, flag_ref[3]

    def chosen(two, four, odd):
        value = jnp.where(distance == 2, two.astype(F32), odd.astype(F32))
        value = jnp.where(distance == 4, four.astype(F32), value)
        return jnp.where(distance == 0, 0.0, value)

    fill_second(
        lambda row: first_ref[row] + chosen(prior_a_ref[row], prior_b_ref[row], prior_c_ref[row]),
        gain2_ref[...], first_row, stage_ref, strided_ref, 0,
    )
    early = early_ref[...] + conv2_frame(strided_ref, 0, weight2_ref, 0)
    shape = tail_a_ref.shape
    tail = chosen(tail_a_ref[...], tail_b_ref[...], tail_c_ref[...])
    out_ref[0] = (early.reshape(shape) + tail).astype(BF16)
    out_ref[1] = done_ref[...]


def whole(shape):
    return pl.BlockSpec(shape, lambda i: (0,) * len(shape))


def call(kernel, operands, outs, scratch, blocks=None, flops=0):
    specs = [pl.BlockSpec(memory_space=SMEM)]
    for index, operand in enumerate(operands[1:]):
        block = (blocks or {}).get(index + 1)
        specs.append(block if block is not None else whole(operand.shape))
    moved = sum(o.size * o.dtype.itemsize for o in list(operands) + list(outs))
    return pl.pallas_call(
        kernel,
        grid=(1,),
        out_shape=outs,
        in_specs=specs,
        out_specs=[whole(o.shape) for o in outs],
        scratch_shapes=scratch,
        compiler_params=pltpu.CompilerParams(vmem_limit_bytes=40 * 1024 * 1024),
        cost_estimate=pl.CostEstimate(flops=flops, bytes_accessed=moved, transcendentals=0),
    )(*operands)


def row_halo(frames, even, rows):
    low = lax.slice_in_dim(frames, rows - ABOVE, rows, axis=1)
    high = lax.slice_in_dim(frames, 0, ABOVE, axis=1)
    pair = swapped(jnp.where(even, low, high), "row", 0)
    cross = swapped(jnp.where(even, high, low), "row", 1)
    return pair, cross


def per_device(
    video_frames, pred_owner, frame_counts, norm1_gain, conv1_weight, conv1_bias, norm2_gain,
    conv2_weight, conv2_bias,
):
    frames, rows, width, channels = video_frames.shape
    wide = conv2_weight.shape[-1]
    half = width // 2
    position = lax.axis_index("group")
    band = lax.axis_index("row")
    distance = jnp.where(pred_owner >= 0, position - pred_owner, 0)
    even = band % 2 == 0
    even_group = position % 2 == 0
    keep = frame_counts >= frames
    flags = jnp.concatenate(
        [jnp.stack([even, band == 0]).astype(jnp.int32), keep.astype(jnp.int32), distance]
    )
    gain1, bias1 = norm1_gain[None], conv1_bias[None]
    gain2, bias2 = norm2_gain[None], conv2_bias[None]
    weight1 = conv1_weight.reshape(3, 3, 3 * channels, channels)
    weight2 = conv2_weight.reshape(3, 3, 3 * channels, wide)

    wanted = swapped(distance, "group", 0)[0]

    def for_partner(own, near, far):
        one = jnp.where(even_group, own, near)
        three = jnp.where(even_group, near, far)
        return jnp.where(wanted == 1, one, three)

    pair, cross = row_halo(video_frames, even, rows)
    own_a = lax.slice_in_dim(video_frames, frames - 1, frames, axis=0)
    near_a = shifted(own_a, "group", 2)
    far_a = shifted(near_a, "group", 2)
    odd_a = swapped(for_partner(own_a, near_a, far_a), "group", 0)

    def window(count, rows_of):
        return VMEM((count, rows_of, width, 3 * channels), BF16)

    stage = VMEM((rows + 1, width + 16, channels), F32)
    strided = VMEM((1, rows + 1, half, 3 * channels), BF16)
    total = VMEM((rows + 1, width, channels), F32)
    band_out = jax.ShapeDtypeStruct((rows + 1, width, channels), BF16)
    band_f32 = jax.ShapeDtypeStruct((rows + 1, width, channels), F32)
    code_out = jax.ShapeDtypeStruct((rows // 2, half, wide), BF16)
    code_f32 = jax.ShapeDtypeStruct((rows // 2 * half, wide), F32)
    one_tap = 2 * (rows + 1) * width * 9 * channels * channels
    one_code = 2 * (rows // 2) * half * 9 * channels * wide
    step2 = pl.BlockSpec((1, 3, 3 * channels, wide), lambda i: (0, 0, 0, 0))
    step2_mid = pl.BlockSpec((1, 3, 3 * channels, wide), lambda i: (1, 0, 0, 0))

    own_b, own_e, strided3 = call(
        send_kernel,
        [flags, video_frames, pair, cross, gain1, weight1, bias1, gain2, weight2],
        [band_out, code_out, jax.ShapeDtypeStruct(strided.shape, BF16)],
        [window(3, rows + 3), stage, total],
        {8: step2},
        flops=4 * one_tap + one_code,
    )
    near_b = shifted(own_b, "group", 2)
    near_e = shifted(own_e, "group", 2)
    first, following, late = call(
        own_kernel,
        [flags, video_frames, pair, cross, gain1, weight1, bias1, gain2, weight2, bias2, strided3],
        [band_f32, band_f32, code_f32],
        [window(3, rows + 3), stage, strided, total],
        flops=6 * one_tap + 2 * one_code,
    )
    far_b = shifted(near_b, "group", 2)
    far_e = shifted(near_e, "group", 2)
    gap = distance[0]
    prior = jnp.where(gap == 2, near_a, jnp.where(gap == 4, far_a, odd_a))
    prior = jnp.where(gap == 0, jnp.zeros_like(prior), prior)
    prior_pair, prior_cross = row_halo(prior, even, rows)
    done, first, early = call(
        next_kernel,
        [flags, prior, prior_pair, prior_cross, gain1, weight1, gain2, weight2, bias2, first,
         following, late],
        [code_out, band_f32, code_f32],
        [window(1, rows + 3), stage, strided, total],
        flops=2 * one_tap + 2 * one_code,
    )
    odd_b = swapped(for_partner(own_b, near_b, far_b), "group", 0)
    odd_e = swapped(for_partner(own_e, near_e, far_e), "group", 0)
    return call(
        last_kernel,
        [flags, near_b, far_b, odd_b, near_e, far_e, odd_e, gain2, weight2, first, early, done],
        [jax.ShapeDtypeStruct((frames // 2, rows // 2, half, wide), BF16)],
        [stage, strided],
        {8: step2_mid},
        flops=one_code,
    )[0]


def solution(mesh):
    placed = (P("group", "row", None, None), P("group"), P("group"), P(), P(), P(), P(), P(), P())
    return jax.shard_map(
        per_device,
        mesh=mesh,
        in_specs=placed,
        out_specs=P("group", "row", None, None),
        check_vma=False,
    )
```

```python
import functools

import jax
import jax.numpy as jnp
from jax import lax
from jax.experimental import pallas as pl
from jax.experimental.pallas import tpu as pltpu
from jax.sharding import PartitionSpec as P

ABOVE = 2
VMEM = pltpu.VMEM
SMEM = pltpu.SMEM
F32 = jnp.float32
BF16 = jnp.bfloat16


def rotated(value, axis, steps):
    count = lax.axis_size(axis)
    return lax.ppermute(value, axis, [(source, (source + steps) % count) for source in range(count)])


def swapped(value, axis, offset):
    count = lax.axis_size(axis)
    pairs = []
    for low in range(offset, count, 2):
        high = (low + 1) % count
        pairs += [(low, high), (high, low)]
    return lax.ppermute(value, axis, pairs)


def pixel_silu(values, gain):
    inverse = lax.rsqrt(jnp.mean(values * values, axis=-1, keepdims=True) + 1e-06)
    half = values * inverse * (0.5 * gain)
    return half + half * jnp.tanh(half)


def column_window(row):
    width = row.shape[0]
    column = lax.broadcasted_iota(jnp.int32, row.shape, 0)
    left = jnp.where(column == 0, 0.0, pltpu.roll(row, 1, 0))
    right = jnp.where(column == width - 1, 0.0, pltpu.roll(row, width - 1, 0))
    return jnp.concatenate([left.astype(BF16), row.astype(BF16), right.astype(BF16)], axis=-1)


def fill_hidden(read, gain, window_ref, frame, rows):
    for row in range(rows):
        window_ref[frame, row] = column_window(pixel_silu(read(row), gain))


def conv1_rows(window_ref, frame, rows, weight):
    width, depth = window_ref.shape[2], window_ref.shape[3]
    total = None
    for tap in range(3):
        part = jnp.dot(
            window_ref[frame, tap : tap + rows].reshape(rows * width, depth),
            weight(tap),
            preferred_element_type=F32,
        )
        total = part if total is None else total + part
    return total


def fill_second(values, gain, first_row, stage_ref, strided_ref, slot):
    rows, half = strided_ref.shape[1], strided_ref.shape[2]
    width, channels = 2 * half, stage_ref.shape[2]
    for row in range(rows):
        ready = pixel_silu(values(row), gain).astype(BF16).astype(F32)
        if row == 0:
            ready = jnp.where(first_row, 0.0, ready)
        stage_ref[row, 0:8] = jnp.zeros((8, channels), F32)
        stage_ref[row, 8 : 8 + width] = ready
        strided_ref[slot, row] = jnp.concatenate(
            [stage_ref[row, pl.ds(7 + tap, half, stride=2), :].astype(BF16) for tap in range(3)],
            axis=-1,
        )


def conv2_frame(strided_ref, slot, weight_ref, step):
    total = None
    for tap in range(3):
        window = jnp.concatenate([strided_ref[slot, tap], strided_ref[slot, tap + 2]], axis=0)
        part = jnp.dot(window, weight_ref[step, tap], preferred_element_type=F32)
        total = part if total is None else total + part
    return total


def row_reader(flag_ref, video_ref, frame, pair_ref, cross_ref):
    even, top, bottom = flag_ref[0] == 1, flag_ref[1] == 1, flag_ref[4] == 1
    rows = video_ref.shape[1]

    def read(row):
        if ABOVE <= row < ABOVE + rows:
            return video_ref[frame, row - ABOVE].astype(F32)
        if row < ABOVE:
            first, second, outside = cross_ref[frame, row], pair_ref[frame, row], top
        else:
            first, second, outside = pair_ref[frame, 0], cross_ref[frame, 0], bottom
        value = jnp.where(even, first.astype(F32), second.astype(F32))
        return jnp.where(outside, 0.0, value)

    return read


def send_kernel(
    flag_ref, video_ref, pair_ref, cross_ref, gain1_ref, weight1_ref, bias1_ref, gain2_ref,
    weight2_ref, prior_ref, tail_ref, strided_out_ref, window_ref, stage_ref, total_ref,
):
    first_row = flag_ref[1] == 1
    channels = video_ref.shape[3]
    readers = [row_reader(flag_ref, video_ref, f, pair_ref, cross_ref) for f in range(4)]
    for slot, frame in enumerate((1, 2, 3)):
        fill_hidden(readers[frame], gain1_ref[...], window_ref, slot, 7)
    both = conv1_rows(
        window_ref, 1, 5,
        lambda tap: jnp.concatenate([weight1_ref[1, tap], weight1_ref[0, tap]], axis=-1),
    )
    prior_ref[...] = both[:, channels:].astype(BF16).reshape(prior_ref.shape)
    total_ref[...] = (
        both[:, :channels]
        + conv1_rows(window_ref, 0, 5, lambda tap: weight1_ref[0, tap])
        + conv1_rows(window_ref, 2, 5, lambda tap: weight1_ref[2, tap])
    ).reshape(total_ref.shape)
    fill_second(
        lambda row: total_ref[row] + readers[3](row + 1) + bias1_ref[...],
        gain2_ref[...], first_row, stage_ref, strided_out_ref, 0,
    )
    tail_ref[...] = conv2_frame(strided_out_ref, 0, weight2_ref, 0).astype(BF16).reshape(tail_ref.shape)


def own_kernel(
    flag_ref, video_ref, pair_ref, cross_ref, gain1_ref, weight1_ref, bias1_ref, gain2_ref,
    weight2_ref, bias2_ref, strided3_ref, first_ref, next_ref, late_ref,
    window_ref, stage_ref, strided_ref, total_ref,
):
    first_row = flag_ref[1] == 1
    channels = video_ref.shape[3]
    readers = [row_reader(flag_ref, video_ref, f, pair_ref, cross_ref) for f in range(4)]
    for frame in range(3):
        fill_hidden(readers[frame], gain1_ref[...], window_ref, frame, 7)
    both = conv1_rows(
        window_ref, 0, 5,
        lambda tap: jnp.concatenate([weight1_ref[0, tap], weight1_ref[1, tap]], axis=-1),
    ) + conv1_rows(
        window_ref, 1, 5,
        lambda tap: jnp.concatenate([weight1_ref[1, tap], weight1_ref[2, tap]], axis=-1),
    )
    next_ref[...] = both[:, channels:].reshape(next_ref.shape)
    total_ref[...] = (
        both[:, :channels] + conv1_rows(window_ref, 2, 5, lambda tap: weight1_ref[2, tap])
    ).reshape(total_ref.shape)
    first_ref[...] = conv1_rows(window_ref, 0, 5, lambda tap: weight1_ref[2, tap]).reshape(first_ref.shape)
    for row in range(5):
        next_ref[row] += readers[1](row + 1) + bias1_ref[...]
        first_ref[row] += readers[0](row + 1) + bias1_ref[...]
    fill_second(
        lambda row: total_ref[row] + readers[2](row + 1) + bias1_ref[...],
        gain2_ref[...], first_row, stage_ref, strided_ref, 0,
    )
    late_ref[...] = (
        conv2_frame(strided_ref, 0, weight2_ref, 1)
        + conv2_frame(strided3_ref, 0, weight2_ref, 2)
        + bias2_ref[...]
    )


def next_kernel(
    flag_ref, prior_ref, pair_ref, cross_ref, gain1_ref, weight1_ref, gain2_ref,
    weight2_ref, bias2_ref, first_ref, next_ref, late_ref, second_out_ref, first_out_ref, early_ref,
    window_ref, stage_ref, strided_ref, total_ref,
):
    first_row, keep = flag_ref[1] == 1, flag_ref[2] == 1
    channels = prior_ref.shape[3]
    fill_hidden(
        row_reader(flag_ref, prior_ref, 0, pair_ref, cross_ref), gain1_ref[...], window_ref, 0, 7
    )
    both = conv1_rows(
        window_ref, 0, 5,
        lambda tap: jnp.concatenate([weight1_ref[0, tap], weight1_ref[1, tap]], axis=-1),
    )
    total_ref[...] = both[:, :channels].reshape(total_ref.shape)
    first_out_ref[...] = first_ref[...] + both[:, channels:].reshape(first_ref.shape)
    fill_second(
        lambda row: total_ref[row] + next_ref[row],
        gain2_ref[...], first_row, stage_ref, strided_ref, 0,
    )
    late = late_ref[...] + conv2_frame(strided_ref, 0, weight2_ref, 0)
    second_out_ref[...] = jnp.where(keep, late, 0.0).astype(BF16).reshape(second_out_ref.shape)
    early_ref[...] = conv2_frame(strided_ref, 0, weight2_ref, 2) + bias2_ref[...]


def last_kernel(
    flag_ref, prior_a_ref, prior_b_ref, prior_c_ref, tail_a_ref, tail_b_ref, tail_c_ref,
    gain2_ref, weight2_ref, first_ref, early_ref, done_ref, out_ref, stage_ref, strided_ref,
):
    first_row, distance = flag_ref[1] == 1, flag_ref[3]

    def chosen(two, four, odd):
        value = jnp.where(distance == 2, two.astype(F32), odd.astype(F32))
        value = jnp.where(distance == 4, four.astype(F32), value)
        return jnp.where(distance == 0, 0.0, value)

    fill_second(
        lambda row: first_ref[row] + chosen(prior_a_ref[row], prior_b_ref[row], prior_c_ref[row]),
        gain2_ref[...], first_row, stage_ref, strided_ref, 0,
    )
    early = early_ref[...] + conv2_frame(strided_ref, 0, weight2_ref, 0)
    shape = tail_a_ref.shape
    tail = chosen(tail_a_ref[...], tail_b_ref[...], tail_c_ref[...])
    out_ref[0] = (early.reshape(shape) + tail).astype(BF16)
    out_ref[1] = done_ref[...]


def pack_kernel(flag_ref, video_ref, own_ref, pair_ref, cross_ref):
    even = flag_ref[0] == 1
    frames, rows = video_ref.shape[:2]
    own_ref[0] = video_ref[frames - 1]
    for frame in range(frames):
        for row in range(ABOVE):
            high, low = video_ref[frame, row], video_ref[frame, rows - ABOVE + row]
            pair_ref[frame, row] = jnp.where(even, low, high)
            cross_ref[frame, row] = jnp.where(even, high, low)


def whole(shape):
    return pl.BlockSpec(shape, lambda i: (0,) * len(shape))


def call(kernel, operands, outs, scratch, blocks=None, flops=0):
    specs = [pl.BlockSpec(memory_space=SMEM)]
    for index, operand in enumerate(operands[1:]):
        block = (blocks or {}).get(index + 1)
        specs.append(block if block is not None else whole(operand.shape))
    moved = sum(o.size * o.dtype.itemsize for o in list(operands) + list(outs))
    return pl.pallas_call(
        kernel,
        grid=(1,),
        out_shape=outs,
        in_specs=specs,
        out_specs=[whole(o.shape) for o in outs],
        scratch_shapes=scratch,
        compiler_params=pltpu.CompilerParams(vmem_limit_bytes=40 * 1024 * 1024),
        cost_estimate=pl.CostEstimate(flops=flops, bytes_accessed=moved, transcendentals=0),
    )(*operands)


def row_halo(frames, even, rows):
    low = lax.slice_in_dim(frames, rows - ABOVE, rows, axis=1)
    high = lax.slice_in_dim(frames, 0, ABOVE, axis=1)
    pair = swapped(jnp.where(even, low, high), "row", 0)
    cross = swapped(jnp.where(even, high, low), "row", 1)
    return pair, cross


def per_device(
    video_frames, pred_owner, frame_counts, norm1_gain, conv1_weight, conv1_bias, norm2_gain,
    conv2_weight, conv2_bias,
):
    frames, rows, width, channels = video_frames.shape
    wide = conv2_weight.shape[-1]
    half = width // 2
    position = lax.axis_index("group")
    band = lax.axis_index("row")
    distance = jnp.where(pred_owner >= 0, position - pred_owner, 0)
    even = band % 2 == 0
    even_group = position % 2 == 0
    keep = frame_counts >= frames
    flags = jnp.concatenate(
        [
            jnp.stack([even, band == 0]).astype(jnp.int32),
            keep.astype(jnp.int32),
            distance,
            (band == lax.axis_size("row") - 1).astype(jnp.int32)[None],
        ]
    )
    gain1, bias1 = norm1_gain[None], conv1_bias[None]
    gain2, bias2 = norm2_gain[None], conv2_bias[None]
    weight1 = conv1_weight.reshape(3, 3, 3 * channels, channels)
    weight2 = conv2_weight.reshape(3, 3, 3 * channels, wide)

    wanted = swapped(distance, "group", 0)[0]

    def for_partner(own, near, far):
        one = jnp.where(even_group, own, near)
        three = jnp.where(even_group, near, far)
        return jnp.where(wanted == 1, one, three)

    edge = jax.ShapeDtypeStruct((frames, ABOVE, width, channels), BF16)
    own_a, pair, cross = call(
        pack_kernel,
        [flags, video_frames],
        [jax.ShapeDtypeStruct((1, rows, width, channels), BF16), edge, edge],
        [],
    )
    pair, cross = swapped(pair, "row", 0), swapped(cross, "row", 1)
    near_a = rotated(own_a, "group", 2)
    far_a = rotated(near_a, "group", 2)
    odd_a = swapped(for_partner(own_a, near_a, far_a), "group", 0)

    def window(count, rows_of):
        return VMEM((count, rows_of, width, 3 * channels), BF16)

    stage = VMEM((rows + 1, width + 16, channels), F32)
    strided = VMEM((1, rows + 1, half, 3 * channels), BF16)
    total = VMEM((rows + 1, width, channels), F32)
    band_out = jax.ShapeDtypeStruct((rows + 1, width, channels), BF16)
    band_f32 = jax.ShapeDtypeStruct((rows + 1, width, channels), F32)
    code_out = jax.ShapeDtypeStruct((rows // 2, half, wide), BF16)
    code_f32 = jax.ShapeDtypeStruct((rows // 2 * half, wide), F32)
    one_tap = 2 * (rows + 1) * width * 9 * channels * channels
    one_code = 2 * (rows // 2) * half * 9 * channels * wide
    step2 = pl.BlockSpec((1, 3, 3 * channels, wide), lambda i: (0, 0, 0, 0))
    step2_mid = pl.BlockSpec((1, 3, 3 * channels, wide), lambda i: (1, 0, 0, 0))

    own_b, own_e, strided3 = call(
        send_kernel,
        [flags, video_frames, pair, cross, gain1, weight1, bias1, gain2, weight2],
        [band_out, code_out, jax.ShapeDtypeStruct(strided.shape, BF16)],
        [window(3, rows + 3), stage, total],
        {8: step2},
        flops=4 * one_tap + one_code,
    )
    near_b = rotated(own_b, "group", 2)
    near_e = rotated(own_e, "group", 2)
    first, following, late = call(
        own_kernel,
        [flags, video_frames, pair, cross, gain1, weight1, bias1, gain2, weight2, bias2, strided3],
        [band_f32, band_f32, code_f32],
        [window(3, rows + 3), stage, strided, total],
        flops=6 * one_tap + 2 * one_code,
    )
    near_b, near_e, first = lax.optimization_barrier((near_b, near_e, first))
    far_b = rotated(near_b, "group", 2)
    far_e = rotated(near_e, "group", 2)
    gap = distance[0]
    prior = jnp.where(gap == 2, near_a, jnp.where(gap == 4, far_a, odd_a))
    prior = jnp.where(gap == 0, jnp.zeros_like(prior), prior)
    prior_pair, prior_cross = row_halo(prior, even, rows)
    done, first, early = call(
        next_kernel,
        [flags, prior, prior_pair, prior_cross, gain1, weight1, gain2, weight2, bias2, first,
         following, late],
        [code_out, band_f32, code_f32],
        [window(1, rows + 3), stage, strided, total],
        flops=2 * one_tap + 2 * one_code,
    )
    odd_b = swapped(for_partner(own_b, near_b, far_b), "group", 0)
    odd_e = swapped(for_partner(own_e, near_e, far_e), "group", 0)
    return call(
        last_kernel,
        [flags, near_b, far_b, odd_b, near_e, far_e, odd_e, gain2, weight2, first, early, done],
        [jax.ShapeDtypeStruct((frames // 2, rows // 2, half, wide), BF16)],
        [stage, strided],
        {8: step2_mid},
        flops=one_code,
    )[0]


def solution(mesh):
    placed = (P("group", "row", None, None), P("group"), P("group"), P(), P(), P(), P(), P(), P())
    return jax.shard_map(
        per_device,
        mesh=mesh,
        in_specs=placed,
        out_specs=P("group", "row", None, None),
        check_vma=False,
    )
```

```python
import functools

import jax
import jax.numpy as jnp
from jax import lax
from jax.experimental import pallas as pl
from jax.experimental.pallas import tpu as pltpu
from jax.sharding import PartitionSpec as P

ABOVE = 2
EVEN, TOP, FULL, DISTANCE, BOTTOM, EVEN_GROUP = range(6)
PACK = 30_000_000_000
VMEM = pltpu.VMEM
F32 = jnp.float32
BF16 = jnp.bfloat16


def rotated(value, axis, steps):
    count = lax.axis_size(axis)
    return lax.ppermute(value, axis, [(source, (source + steps) % count) for source in range(count)])


def relayed(value):
    groups, rows = lax.axis_size("group"), lax.axis_size("row")
    pairs = []
    for group in range(groups):
        for row in range(rows):
            if group < 2:
                target = (group, row ^ 1)
            else:
                target = (group + 2 if group + 2 < groups else group + 4 - groups, row)
            pairs.append((group * rows + row, target[0] * rows + target[1]))
    return lax.ppermute(value, ("group", "row"), pairs)


def swapped(value, axis):
    return lax.ppermute(value, axis, [(place, place ^ 1) for place in range(lax.axis_size(axis))])


def crossed_within(value):
    rows = lax.axis_size("row")
    return lax.ppermute(
        value, "row", [(row, (((row + 1) ^ 1) - 1) % rows) for row in range(rows)]
    )


def crossed(value):
    groups, rows = lax.axis_size("group"), lax.axis_size("row")
    pairs = []
    for group in range(groups):
        for row in range(rows):
            outer = row in (0, rows - 1)
            target = (group ^ 1, row) if outer else (group, ((row + 1) ^ 1) - 1)
            pairs.append((group * rows + row, target[0] * rows + target[1]))
    return lax.ppermute(value, ("group", "row"), pairs)


def after(first, *values):
    return lax.optimization_barrier((first,) + values)[1:]


def pixel_silu(values, gain):
    inverse = lax.rsqrt(jnp.mean(values * values, axis=-1, keepdims=True) + 1e-06)
    half = values * inverse * (0.5 * gain)
    return half + half * jnp.tanh(half)


def column_window(row):
    width = row.shape[0]
    column = lax.broadcasted_iota(jnp.int32, row.shape, 0)
    left = jnp.where(column == 0, 0.0, pltpu.roll(row, 1, 0))
    right = jnp.where(column == width - 1, 0.0, pltpu.roll(row, width - 1, 0))
    return jnp.concatenate([left.astype(BF16), row.astype(BF16), right.astype(BF16)], axis=-1)


def holds(flag_ref, index):
    return flag_ref[index : index + 1] != 0


def fill_hidden(read, gain, window_ref, frame, rows):
    for row in rows:
        window_ref[frame, row] = column_window(pixel_silu(read(row), gain))


def conv1_rows(window_ref, frame, rows, weight):
    width, depth = window_ref.shape[2], window_ref.shape[3]
    window = jnp.concatenate(
        [window_ref[frame, tap : tap + rows].reshape(rows * width, depth) for tap in range(3)],
        axis=-1,
    )
    return jnp.dot(window, weight.reshape(3 * depth, weight.shape[2]), preferred_element_type=F32)


def fill_second(values, gain, first_row, stage_ref, strided_ref, slot):
    rows, half = strided_ref.shape[1], strided_ref.shape[2]
    width, channels = 2 * half, stage_ref.shape[2]
    for row in range(rows):
        ready = pixel_silu(values(row), gain).astype(BF16).astype(F32)
        if row == 0:
            ready = jnp.where(first_row, 0.0, ready)
        stage_ref[row, 0:8] = jnp.zeros((8, channels), F32)
        stage_ref[row, 8 : 8 + width] = ready
        strided_ref[slot, row] = jnp.concatenate(
            [stage_ref[row, pl.ds(7 + tap, half, stride=2), :].astype(BF16) for tap in range(3)],
            axis=-1,
        )


def conv2_frame(strided_ref, slot, weight_ref, step):
    total = None
    for tap in range(3):
        window = jnp.concatenate([strided_ref[slot, tap], strided_ref[slot, tap + 2]], axis=0)
        part = jnp.dot(window, weight_ref[step, tap], preferred_element_type=F32)
        total = part if total is None else total + part
    return total


def row_reader(flag_ref, video_ref, frame, pair_ref, cross_ref):
    even, top, bottom = holds(flag_ref, EVEN), holds(flag_ref, TOP), holds(flag_ref, BOTTOM)
    rows = video_ref.shape[1]

    def read(row):
        if ABOVE <= row < ABOVE + rows:
            return video_ref[frame, row - ABOVE].astype(F32)
        if row < ABOVE:
            first, second, outside = cross_ref[frame, row], pair_ref[frame, row], top
        else:
            first, second, outside = pair_ref[frame, 0], cross_ref[frame, 0], bottom
        value = jnp.where(even, first.astype(F32), second.astype(F32))
        return jnp.where(outside, 0.0, value)

    return read


def pack_kernel(flag_ref, video_ref, own_ref, pair_ref, cross_ref):
    even = holds(flag_ref, EVEN)
    frames, rows = video_ref.shape[:2]
    own_ref[...] = video_ref[frames - 2 :]
    split_edges(even, video_ref, frames, rows, pair_ref, cross_ref)


def split_edges(even, source_ref, frames, rows, pair_ref, cross_ref):
    for frame in range(frames):
        for row in range(ABOVE):
            high, low = source_ref[frame, row], source_ref[frame, rows - ABOVE + row]
            pair_ref[frame, row] = jnp.where(even, low, high)
            cross_ref[frame, row] = jnp.where(even, high, low)


def beside(weight_ref, *steps):
    return jnp.concatenate([weight_ref[step] for step in steps], axis=-1)


def own_kernel(
    flag_ref, video_ref, pair_ref, cross_ref, gain1_ref, weight1_ref, bias1_ref,
    gain2_ref, weight2_ref, bias2_ref, tail_ref, first_ref, next_ref, late_ref,
    window_ref, stage_ref, strided_ref, total_ref,
):
    first_row = holds(flag_ref, TOP)
    channels = video_ref.shape[3]
    readers = [row_reader(flag_ref, video_ref, f, pair_ref, cross_ref) for f in range(4)]
    for frame in range(4):
        fill_hidden(readers[frame], gain1_ref[...], window_ref, frame, range(7))
    zero = conv1_rows(window_ref, 0, 5, beside(weight1_ref, 0, 1))
    one = conv1_rows(window_ref, 1, 5, beside(weight1_ref, 1, 2))
    two = conv1_rows(window_ref, 2, 5, beside(weight1_ref, 2, 1))
    next_ref[...] = (zero[:, channels:] + one[:, channels:]).reshape(next_ref.shape)
    total_ref[0] = (zero[:, :channels] + one[:, :channels] + two[:, :channels]).reshape(next_ref.shape)
    total_ref[1] = (
        two[:, channels:]
        + conv1_rows(window_ref, 1, 5, weight1_ref[0])
        + conv1_rows(window_ref, 3, 5, weight1_ref[2])
    ).reshape(next_ref.shape)
    first_ref[...] = conv1_rows(window_ref, 0, 5, weight1_ref[2]).reshape(first_ref.shape)
    for row in range(5):
        next_ref[row] += readers[1](row + 1) + bias1_ref[...]
        first_ref[row] += readers[0](row + 1) + bias1_ref[...]
    for slot in range(2):
        fill_second(
            lambda row: total_ref[slot, row] + readers[2 + slot](row + 1) + bias1_ref[...],
            gain2_ref[...], first_row, stage_ref, strided_ref, slot,
        )
    late_ref[...] = (
        conv2_frame(strided_ref, 0, weight2_ref, 1)
        + conv2_frame(strided_ref, 1, weight2_ref, 2)
        + bias2_ref[...]
    )
    tail = conv2_frame(strided_ref, 1, weight2_ref, 0).astype(BF16)
    half = strided_ref.shape[2]
    for row in range(tail_ref.shape[0]):
        for part in range(2):
            tail_ref[row, part * half : (part + 1) * half] = tail[
                row * half : (row + 1) * half, part * channels : (part + 1) * channels
            ]


def chosen(distance, two, four, odd):
    value = jnp.where(distance == 2, two, odd)
    value = jnp.where(distance == 4, four, value)
    return jnp.where(distance == 0, 0.0, value)


def partner_kernel(flag_ref, wanted_ref, own_ref, near_ref, far_ref, out_ref):
    first, one = holds(flag_ref, EVEN_GROUP), wanted_ref[0:1] == 1
    for row in range(out_ref.shape[0]):
        own, near, far = own_ref[row], near_ref[row], far_ref[row]
        out_ref[row] = jnp.where(
            first, jnp.where(one, own, near), jnp.where(one, near, far)
        )


def prior_kernel(
    flag_ref, two_ref, four_ref, odd_ref, prior_ref, pair_ref, cross_ref,
):
    even, distance = holds(flag_ref, EVEN), flag_ref[DISTANCE : DISTANCE + 1]
    frames, rows = prior_ref.shape[:2]
    for frame in range(frames):
        for row in range(rows):
            at = frame * rows + row
            prior_ref[frame, row] = chosen(distance, two_ref[at], four_ref[at], odd_ref[at])
    split_edges(even, prior_ref, frames, rows, pair_ref, cross_ref)


def inner_kernel(
    flag_ref, prior_ref, gain1_ref, weight1_ref, first_ref, next_ref, first_out_ref, next_out_ref,
    window_ref,
):
    del flag_ref
    rows, width, channels = prior_ref.shape[1:]
    for frame in range(2):
        fill_hidden(
            lambda row: prior_ref[frame, row].astype(F32), gain1_ref[...], window_ref, frame, range(rows)
        )
    first_out_ref[...] = first_ref[...]
    next_out_ref[...] = next_ref[...]
    for tap in range(3):
        low = max(0, ABOVE - tap)
        count = min(rows + 1, rows + ABOVE - tap) - low
        start = low + tap - ABOVE
        shape = (count, width, channels)

        def part(frame, weight):
            window = window_ref[frame, start : start + count]
            return jnp.dot(
                window.reshape(count * width, window.shape[2]), weight, preferred_element_type=F32
            )

        both = part(1, beside(weight1_ref.at[:, tap], 0, 1))
        next_out_ref[low : low + count] += both[:, :channels].reshape(shape)
        first_out_ref[low : low + count] += (
            both[:, channels:] + part(0, weight1_ref[0, tap])
        ).reshape(shape)


def last_kernel(
    flag_ref, prior_ref, pair_ref, cross_ref, gain1_ref, weight1_ref, gain2_ref,
    weight2_ref, bias2_ref, first_ref, next_ref, late_ref, two_ref, four_ref, odd_ref, out_ref,
    window_ref, stage_ref, strided_ref, total_ref,
):
    first_row, keep, distance = holds(flag_ref, TOP), holds(flag_ref, FULL), flag_ref[DISTANCE : DISTANCE + 1]
    rows, width, channels = prior_ref.shape[1:]
    outer = (0, 1, rows + ABOVE)
    for frame in range(2):
        reader = row_reader(flag_ref, prior_ref, frame, pair_ref, cross_ref)
        fill_hidden(
            lambda slot: reader(outer[slot]), gain1_ref[...], window_ref, frame, range(len(outer))
        )
    total_ref[0] = next_ref[...]
    total_ref[1] = first_ref[...]
    for slot, place in enumerate(outer):
        for tap in range(3):
            target = place - tap
            if 0 <= target <= rows:
                both = jnp.dot(
                    window_ref[1, slot], beside(weight1_ref.at[:, tap], 0, 1), preferred_element_type=F32
                )
                total_ref[0, target] += both[:, :channels]
                total_ref[1, target] += both[:, channels:] + jnp.dot(
                    window_ref[0, slot], weight1_ref[0, tap], preferred_element_type=F32
                )
    for slot in range(2):
        fill_second(
            lambda row: total_ref[slot, row],
            gain2_ref[...], first_row, stage_ref, strided_ref, slot,
        )
    shape = out_ref.shape[1:]
    half = strided_ref.shape[2]
    late = late_ref[...] + conv2_frame(strided_ref, 0, weight2_ref, 0)
    out_ref[1] = jnp.where(jnp.concatenate([keep, keep], axis=-1), late, 0.0).astype(BF16).reshape(shape)
    early = conv2_frame(strided_ref, 0, weight2_ref, 2) + conv2_frame(strided_ref, 1, weight2_ref, 1)
    for row in range(shape[0]):
        tail = chosen(
            distance, two_ref[row].astype(F32), four_ref[row].astype(F32), odd_ref[row].astype(F32)
        )
        tail = jnp.concatenate([tail[:half], tail[half:]], axis=-1)
        part = early[row * half : (row + 1) * half] + bias2_ref[...]
        out_ref[0, row] = (part + tail).astype(BF16)


def call(kernel, operands, outs, scratch, flops=0):
    moved = sum(o.size * o.dtype.itemsize for o in list(operands) + list(outs))
    return pl.pallas_call(
        kernel,
        out_shape=outs,
        in_specs=[pl.BlockSpec(memory_space=VMEM)] * len(operands),
        out_specs=[pl.BlockSpec(memory_space=VMEM)] * len(outs),
        scratch_shapes=scratch,
        compiler_params=pltpu.CompilerParams(vmem_limit_bytes=14 * 1024 * 1024),
        cost_estimate=pl.CostEstimate(flops=flops, bytes_accessed=moved, transcendentals=0),
    )(*operands)


def per_device(
    video_frames, pred_owner, frame_counts, norm1_gain, conv1_weight, conv1_bias, norm2_gain,
    conv2_weight, conv2_bias,
):
    frames, rows, width, channels = video_frames.shape
    wide = conv2_weight.shape[-1]
    half = width // 2
    position = lax.axis_index("group")
    band = lax.axis_index("row")
    distance = jnp.where(pred_owner[0] >= 0, position - pred_owner[0], 0)
    marks = [
        band % 2 == 0, band == 0, frame_counts[0] >= frames, distance,
        band == lax.axis_size("row") - 1, position % 2 == 0,
    ]
    marks += [0] * (8 - len(marks))
    flags = jnp.stack([jnp.full((channels,), mark, F32) for mark in marks])

    def like(value, dtype=BF16):
        return jax.ShapeDtypeStruct(value, dtype)

    def window(count, high):
        return VMEM((count, high, width, 3 * channels), BF16)

    def for_partner(own, near, far):
        return call(partner_kernel, [flags, wanted, own, near, far], [like(own.shape)], [])[0]

    weight1 = conv1_weight.reshape(3, 3, 3 * channels, channels)
    weight2 = conv2_weight.reshape(3, 3, 3 * channels, wide)
    gain1, bias1 = norm1_gain[None], conv1_bias[None]
    gain2, bias2 = norm2_gain[None], conv2_bias[None]
    pair_of = like((2, rows, width, channels))
    flat = (2 * rows, width, channels)
    total = (rows + 1, width, channels)
    stage = VMEM((rows + 1, width + 16, channels), F32)
    strided = VMEM((2, rows + 1, half, 3 * channels), BF16)
    one_tap = 2 * (rows + 1) * width * 9 * channels * channels
    one_code = 2 * (rows // 2) * half * 9 * channels * wide

    edge = like((frames, ABOVE, width, channels))
    own, pair, cross = call(
        pack_kernel, [flags, video_frames], [pair_of, edge, edge], [], flops=PACK
    )
    wanted = swapped(jnp.full((8, channels), distance, F32), "group")
    cross = crossed(after(wanted, cross)[0])
    own = own.reshape(flat)
    near = rotated(own, "group", 2)
    pair = swapped(pair, "row")
    far = relayed(near)
    pair, cross = after(near, pair, cross)
    own_e, first, following, late = call(
        own_kernel,
        [flags, video_frames, pair, cross, gain1, weight1, bias1, gain2, weight2, bias2],
        [
            like((rows // 2, width, channels)), like(total, F32), like(total, F32),
            like((rows // 2 * half, wide), F32),
        ],
        [window(4, rows + 3), stage, strided, VMEM((2,) + total, F32)],
        flops=9 * one_tap + 3 * one_code,
    )
    chosen_own = for_partner(own, near, after(own_e, far)[0])
    odd = swapped(chosen_own, "group")
    near_e = rotated(own_e, "group", 2)
    far_e = relayed(near_e)
    odd_e = swapped(for_partner(own_e, near_e, far_e), "group")
    edge = like((2, ABOVE, width, channels))
    prior, prior_pair, prior_cross = call(
        prior_kernel, [flags, near, far, odd], [pair_of, edge, edge], []
    )
    prior_cross = crossed_within(prior_cross)
    prior_pair = swapped(prior_pair, "row")
    first, following = call(
        inner_kernel,
        [flags, prior, gain1, weight1, first, following],
        [like(total, F32), like(total, F32)],
        [window(2, rows)],
        flops=2 * one_tap,
    )
    return call(
        last_kernel,
        [flags, prior, prior_pair, prior_cross, gain1, weight1, gain2, weight2, bias2, first,
         following, late, near_e, far_e, odd_e],
        [like((frames // 2, rows // 2, half, wide))],
        [window(2, 3), stage, strided, VMEM((2,) + total, F32)],
        flops=one_tap + 3 * one_code,
    )[0]


def solution(mesh):
    placed = (P("group", "row", None, None), P("group"), P("group"), P(), P(), P(), P(), P(), P())
    return jax.shard_map(
        per_device,
        mesh=mesh,
        in_specs=placed,
        out_specs=P("group", "row", None, None),
        check_vma=False,
    )
```

```python
import functools

import jax
import jax.numpy as jnp
from jax import lax
from jax.experimental import pallas as pl
from jax.experimental.pallas import tpu as pltpu
from jax.sharding import PartitionSpec as P

ABOVE = 2
EVEN, TOP, FULL, DISTANCE, BOTTOM, EVEN_GROUP = range(6)
PACK = 30_000_000_000
WHILE_SWAPPED = 4_000_000_000
VMEM = pltpu.VMEM
F32 = jnp.float32
BF16 = jnp.bfloat16


def rotated(value, axis, steps):
    count = lax.axis_size(axis)
    return lax.ppermute(value, axis, [(source, (source + steps) % count) for source in range(count)])


def relayed(value):
    groups, rows = lax.axis_size("group"), lax.axis_size("row")
    pairs = []
    for group in range(groups):
        for row in range(rows):
            if group < 2:
                target = (group, row ^ 1)
            else:
                target = (group + 2 if group + 2 < groups else group + 4 - groups, row)
            pairs.append((group * rows + row, target[0] * rows + target[1]))
    return lax.ppermute(value, ("group", "row"), pairs)


def swapped(value, axis):
    return lax.ppermute(value, axis, [(place, place ^ 1) for place in range(lax.axis_size(axis))])


def crossed_late(value):
    groups, rows = lax.axis_size("group"), lax.axis_size("row")
    planes = groups // 2
    pairs = []
    for group in range(groups):
        plane = group // 2
        for row in range(rows):
            if 0 < row < rows - 1:
                target = (group, ((row + 1) ^ 1) - 1)
            elif 0 < plane < planes - 1 and planes % 2 == 0:
                target = (2 * (((plane + 1) ^ 1) - 1) + group % 2, row)
            else:
                target = (group, rows - 1 - row)
            pairs.append((group * rows + row, target[0] * rows + target[1]))
    return lax.ppermute(value, ("group", "row"), pairs)


def crossed(value):
    groups, rows = lax.axis_size("group"), lax.axis_size("row")
    pairs = []
    for group in range(groups):
        for row in range(rows):
            outer = row in (0, rows - 1)
            target = (group ^ 1, row) if outer else (group, ((row + 1) ^ 1) - 1)
            pairs.append((group * rows + row, target[0] * rows + target[1]))
    return lax.ppermute(value, ("group", "row"), pairs)


def after(first, *values):
    return lax.optimization_barrier((first,) + values)[1:]


def pixel_silu(values, gain):
    inverse = lax.rsqrt(jnp.mean(values * values, axis=-1, keepdims=True) + 1e-06)
    half = values * inverse * (0.5 * gain)
    return half + half * jnp.tanh(half)


def column_window(row):
    width = row.shape[0]
    column = lax.broadcasted_iota(jnp.int32, row.shape, 0)
    left = jnp.where(column == 0, 0.0, pltpu.roll(row, 1, 0))
    right = jnp.where(column == width - 1, 0.0, pltpu.roll(row, width - 1, 0))
    return jnp.concatenate([left.astype(BF16), row.astype(BF16), right.astype(BF16)], axis=-1)


def holds(flag_ref, index):
    return flag_ref[index : index + 1] != 0


def fill_hidden(read, gain, window_ref, frame, rows):
    for row in rows:
        window_ref[frame, row] = column_window(pixel_silu(read(row), gain))


def conv1_rows(window_ref, frame, rows, weight):
    width, depth = window_ref.shape[2], window_ref.shape[3]
    window = jnp.concatenate(
        [window_ref[frame, tap : tap + rows].reshape(rows * width, depth) for tap in range(3)],
        axis=-1,
    )
    return jnp.dot(window, weight.reshape(3 * depth, weight.shape[2]), preferred_element_type=F32)


def fill_second(values, gain, first_row, stage_ref, strided_ref, slot, rows):
    half = strided_ref.shape[2]
    width, channels = 2 * half, stage_ref.shape[2]
    for row in rows:
        ready = pixel_silu(values(row), gain).astype(BF16).astype(F32)
        if row == 0:
            ready = jnp.where(first_row, 0.0, ready)
        stage_ref[row, 0:8] = jnp.zeros((8, channels), F32)
        stage_ref[row, 8 : 8 + width] = ready
        strided_ref[slot, row] = jnp.concatenate(
            [stage_ref[row, pl.ds(7 + tap, half, stride=2), :].astype(BF16) for tap in range(3)],
            axis=-1,
        )


def conv2_frame(weight_ref, *parts):
    windows, weights = [], []
    for strided_ref, slot, step in parts:
        for tap in range(3):
            windows.append(
                jnp.concatenate([strided_ref[slot, tap], strided_ref[slot, tap + 2]], axis=0)
            )
            weights.append(weight_ref[step, tap])
    return jnp.dot(
        jnp.concatenate(windows, axis=-1), jnp.concatenate(weights, axis=0), preferred_element_type=F32
    )


def row_reader(flag_ref, video_ref, frame, pair_ref, cross_ref):
    even, top, bottom = holds(flag_ref, EVEN), holds(flag_ref, TOP), holds(flag_ref, BOTTOM)
    rows = video_ref.shape[1]

    def read(row):
        if ABOVE <= row < ABOVE + rows:
            return video_ref[frame, row - ABOVE].astype(F32)
        if row < ABOVE:
            first, second, outside = cross_ref[frame, row], pair_ref[frame, row], top
        else:
            first, second, outside = pair_ref[frame, 0], cross_ref[frame, 0], bottom
        value = jnp.where(even, first.astype(F32), second.astype(F32))
        return jnp.where(outside, 0.0, value)

    return read


def pack_kernel(flag_ref, video_ref, own_ref, pair_ref, cross_ref):
    even = holds(flag_ref, EVEN)
    frames, rows = video_ref.shape[:2]
    own_ref[...] = video_ref[frames - 2 :]
    split_edges(even, video_ref, frames, rows, pair_ref, cross_ref)


def split_edges(even, source_ref, frames, rows, pair_ref, cross_ref):
    for frame in range(frames):
        for row in range(ABOVE):
            high, low = source_ref[frame, row], source_ref[frame, rows - ABOVE + row]
            pair_ref[frame, row] = jnp.where(even, low, high)
            cross_ref[frame, row] = jnp.where(even, high, low)


def beside(weight_ref, *steps):
    return jnp.concatenate([weight_ref[step] for step in steps], axis=-1)


def send_kernel(
    flag_ref, video_ref, pair_ref, cross_ref, gain1_ref, weight1_ref, bias1_ref,
    gain2_ref, weight2_ref, tail_ref, strided_out_ref, window_ref, stage_ref, total_ref,
):
    first_row = holds(flag_ref, TOP)
    channels = video_ref.shape[3]
    readers = [row_reader(flag_ref, video_ref, f, pair_ref, cross_ref) for f in range(4)]
    for slot, frame in enumerate((1, 2, 3)):
        fill_hidden(readers[frame], gain1_ref[...], window_ref, slot, range(7))
    total_ref[...] = sum(
        conv1_rows(window_ref, step, 5, weight1_ref[step]) for step in range(3)
    ).reshape(total_ref.shape)
    fill_second(
        lambda row: total_ref[row] + readers[3](row + 1) + bias1_ref[...],
        gain2_ref[...], first_row, stage_ref, strided_out_ref, 0, range(5),
    )
    tail = conv2_frame(weight2_ref, (strided_out_ref, 0, 0)).astype(BF16)
    half = strided_out_ref.shape[2]
    for row in range(tail_ref.shape[0]):
        for part in range(2):
            tail_ref[row, part * half : (part + 1) * half] = tail[
                row * half : (row + 1) * half, part * channels : (part + 1) * channels
            ]


def own_kernel(
    flag_ref, video_ref, pair_ref, cross_ref, gain1_ref, weight1_ref, bias1_ref,
    gain2_ref, weight2_ref, bias2_ref, strided3_ref, first_ref, next_ref, late_ref,
    window_ref, stage_ref, strided_ref, total_ref,
):
    first_row = holds(flag_ref, TOP)
    channels = video_ref.shape[3]
    readers = [row_reader(flag_ref, video_ref, f, pair_ref, cross_ref) for f in range(4)]
    for frame in range(3):
        fill_hidden(readers[frame], gain1_ref[...], window_ref, frame, range(7))
    both = conv1_rows(window_ref, 0, 5, beside(weight1_ref, 0, 1))
    both += conv1_rows(window_ref, 1, 5, beside(weight1_ref, 1, 2))
    next_ref[...] = both[:, channels:].reshape(next_ref.shape)
    total_ref[...] = (
        both[:, :channels] + conv1_rows(window_ref, 2, 5, weight1_ref[2])
    ).reshape(next_ref.shape)
    first_ref[...] = conv1_rows(window_ref, 0, 5, weight1_ref[2]).reshape(first_ref.shape)
    for row in range(5):
        next_ref[row] += readers[1](row + 1) + bias1_ref[...]
        first_ref[row] += readers[0](row + 1) + bias1_ref[...]
    fill_second(
        lambda row: total_ref[row] + readers[2](row + 1) + bias1_ref[...],
        gain2_ref[...], first_row, stage_ref, strided_ref, 0, range(5),
    )
    late_ref[...] = (
        conv2_frame(weight2_ref, (strided_ref, 0, 1), (strided3_ref, 0, 2)) + bias2_ref[...]
    )


def chosen(distance, two, four, odd):
    value = jnp.where(distance == 2, two, odd)
    value = jnp.where(distance == 4, four, value)
    return jnp.where(distance == 0, 0.0, value)


def partner_kernel(flag_ref, wanted_ref, own_ref, near_ref, far_ref, out_ref):
    first, one = holds(flag_ref, EVEN_GROUP), wanted_ref[0:1] == 1
    for row in range(out_ref.shape[0]):
        own, near, far = own_ref[row], near_ref[row], far_ref[row]
        out_ref[row] = jnp.where(
            first, jnp.where(one, own, near), jnp.where(one, near, far)
        )


def prior_kernel(
    flag_ref, two_ref, four_ref, odd_ref, prior_ref, pair_ref, cross_ref,
):
    even, distance = holds(flag_ref, EVEN), flag_ref[DISTANCE : DISTANCE + 1]
    frames, rows = prior_ref.shape[:2]
    for frame in range(frames):
        for row in range(rows):
            at = frame * rows + row
            prior_ref[frame, row] = chosen(distance, two_ref[at], four_ref[at], odd_ref[at])
    split_edges(even, prior_ref, frames, rows, pair_ref, cross_ref)


def inner_kernel(
    flag_ref, prior_ref, gain1_ref, weight1_ref, gain2_ref, first_ref, next_ref,
    first_out_ref, next_out_ref, strided_out_ref, window_ref, stage_ref,
):
    del flag_ref
    rows, width, channels = prior_ref.shape[1:]
    for frame in range(2):
        fill_hidden(
            lambda row: prior_ref[frame, row].astype(F32), gain1_ref[...], window_ref, frame, range(rows)
        )
    first_out_ref[...] = first_ref[...]
    next_out_ref[...] = next_ref[...]
    for tap in range(3):
        low = max(0, ABOVE - tap)
        count = min(rows + 1, rows + ABOVE - tap) - low
        start = low + tap - ABOVE
        shape = (count, width, channels)

        def part(frame, weight):
            window = window_ref[frame, start : start + count]
            return jnp.dot(
                window.reshape(count * width, window.shape[2]), weight, preferred_element_type=F32
            )

        both = part(1, beside(weight1_ref.at[:, tap], 0, 1))
        next_out_ref[low : low + count] += both[:, :channels].reshape(shape)
        first_out_ref[low : low + count] += (
            both[:, channels:] + part(0, weight1_ref[0, tap])
        ).reshape(shape)
    for slot, total_ref in enumerate((next_out_ref, first_out_ref)):
        fill_second(
            lambda row: total_ref[row],
            gain2_ref[...], None, stage_ref, strided_out_ref, slot, range(ABOVE, rows),
        )


def side_by_side(window_ref, frame, taps, weight):
    return jnp.dot(
        jnp.concatenate([window_ref[frame, slot] for slot, _ in taps], axis=-1),
        jnp.concatenate([weight[tap] for _, tap in taps], axis=0),
        preferred_element_type=F32,
    )


def last_kernel(
    flag_ref, prior_ref, pair_ref, cross_ref, gain1_ref, weight1_ref, gain2_ref,
    weight2_ref, bias2_ref, first_ref, next_ref, late_ref, inner_ref, two_ref, four_ref, odd_ref, out_ref,
    window_ref, stage_ref, strided_ref, total_ref,
):
    first_row, keep, distance = holds(flag_ref, TOP), holds(flag_ref, FULL), flag_ref[DISTANCE : DISTANCE + 1]
    rows, width, channels = prior_ref.shape[1:]
    outer = (0, 1, rows + ABOVE)
    for frame in range(2):
        reader = row_reader(flag_ref, prior_ref, frame, pair_ref, cross_ref)
        fill_hidden(
            lambda slot: reader(outer[slot]), gain1_ref[...], window_ref, frame, range(len(outer))
        )
    for target in (0, 1, rows):
        taps = [(slot, place - target) for slot, place in enumerate(outer) if 0 <= place - target < 3]
        total_ref[0, target] = next_ref[target]
        total_ref[1, target] = first_ref[target]
        both = side_by_side(window_ref, 1, taps, beside(weight1_ref, 0, 1))
        total_ref[0, target] += both[:, :channels]
        total_ref[1, target] += both[:, channels:] + side_by_side(
            window_ref, 0, taps, weight1_ref[0]
        )
    for slot in range(2):
        strided_ref[slot, ABOVE:rows] = inner_ref[slot, ABOVE:rows]
        fill_second(
            lambda row: total_ref[slot, row],
            gain2_ref[...], first_row, stage_ref, strided_ref, slot, (0, 1, rows),
        )
    shape = out_ref.shape[1:]
    half = strided_ref.shape[2]
    late = late_ref[...] + conv2_frame(weight2_ref, (strided_ref, 0, 0))
    out_ref[1] = jnp.where(jnp.concatenate([keep, keep], axis=-1), late, 0.0).astype(BF16).reshape(shape)
    early = conv2_frame(weight2_ref, (strided_ref, 0, 2), (strided_ref, 1, 1))
    for row in range(shape[0]):
        tail = chosen(
            distance, two_ref[row].astype(F32), four_ref[row].astype(F32), odd_ref[row].astype(F32)
        )
        tail = jnp.concatenate([tail[:half], tail[half:]], axis=-1)
        part = early[row * half : (row + 1) * half] + bias2_ref[...]
        out_ref[0, row] = (part + tail).astype(BF16)


def call(kernel, operands, outs, scratch, flops=0):
    moved = sum(o.size * o.dtype.itemsize for o in list(operands) + list(outs))
    return pl.pallas_call(
        kernel,
        out_shape=outs,
        in_specs=[pl.BlockSpec(memory_space=VMEM)] * len(operands),
        out_specs=[pl.BlockSpec(memory_space=VMEM)] * len(outs),
        scratch_shapes=scratch,
        compiler_params=pltpu.CompilerParams(vmem_limit_bytes=14 * 1024 * 1024),
        cost_estimate=pl.CostEstimate(flops=flops, bytes_accessed=moved, transcendentals=0),
    )(*operands)


def per_device(
    video_frames, pred_owner, frame_counts, norm1_gain, conv1_weight, conv1_bias, norm2_gain,
    conv2_weight, conv2_bias,
):
    frames, rows, width, channels = video_frames.shape
    wide = conv2_weight.shape[-1]
    half = width // 2
    position = lax.axis_index("group")
    band = lax.axis_index("row")
    distance = jnp.where(pred_owner[0] >= 0, position - pred_owner[0], 0)
    marks = [
        band % 2 == 0, band == 0, frame_counts[0] >= frames, distance,
        band == lax.axis_size("row") - 1, position % 2 == 0,
    ]
    marks += [0] * (8 - len(marks))
    flags = jnp.stack([jnp.full((channels,), mark, F32) for mark in marks])

    def like(value, dtype=BF16):
        return jax.ShapeDtypeStruct(value, dtype)

    def window(count, high):
        return VMEM((count, high, width, 3 * channels), BF16)

    def for_partner(own, near, far):
        return call(partner_kernel, [flags, wanted, own, near, far], [like(own.shape)], [])[0]

    weight1 = conv1_weight.reshape(3, 3, 3 * channels, channels)
    weight2 = conv2_weight.reshape(3, 3, 3 * channels, wide)
    gain1, bias1 = norm1_gain[None], conv1_bias[None]
    gain2, bias2 = norm2_gain[None], conv2_bias[None]
    pair_of = like((2, rows, width, channels))
    flat = (2 * rows, width, channels)
    total = (rows + 1, width, channels)
    stage = VMEM((rows + 1, width + 16, channels), F32)
    strided = VMEM((2, rows + 1, half, 3 * channels), BF16)
    one_tap = 2 * (rows + 1) * width * 9 * channels * channels
    one_code = 2 * (rows // 2) * half * 9 * channels * wide

    edge = like((frames, ABOVE, width, channels))
    own, pair, cross = call(
        pack_kernel, [flags, video_frames], [pair_of, edge, edge], [], flops=PACK
    )
    wanted = swapped(jnp.full((8, channels), distance, F32), "group")
    cross = crossed(after(wanted, cross)[0])
    own = own.reshape(flat)
    near = rotated(own, "group", 2)
    pair = swapped(pair, "row")
    far = relayed(near)
    pair, cross = after(near, pair, cross)
    own_e, strided3 = call(
        send_kernel,
        [flags, video_frames, pair, cross, gain1, weight1, bias1, gain2, weight2],
        [like((rows // 2, width, channels)), like((1, rows + 1, half, 3 * channels))],
        [window(3, rows + 3), stage, VMEM(total, F32)],
        flops=3 * one_tap + one_code,
    )
    chosen_own = for_partner(own, near, after(own_e, far)[0])
    odd = swapped(chosen_own, "group")
    near_e = rotated(own_e, "group", 2)
    far_e = relayed(near_e)
    first, following, late = call(
        own_kernel,
        [
            flags, video_frames, pair, cross, gain1, weight1, bias1, gain2, weight2, bias2,
            after(near_e, strided3)[0],
        ],
        [like(total, F32), like(total, F32), like((rows // 2 * half, wide), F32)],
        [window(3, rows + 3), stage, strided, VMEM(total, F32)],
        flops=WHILE_SWAPPED,
    )
    odd_e = swapped(for_partner(own_e, near_e, far_e), "group")
    edge = like((2, ABOVE, width, channels))
    prior, prior_pair, prior_cross = call(
        prior_kernel, [flags, near, far, after(first, odd)[0]], [pair_of, edge, edge], []
    )
    prior_cross = crossed_late(prior_cross)
    prior_pair = swapped(prior_pair, "row")
    first, following, inner = call(
        inner_kernel,
        [flags, prior, gain1, weight1, gain2, first, following],
        [like(total, F32), like(total, F32), like((2, rows + 1, half, 3 * channels))],
        [window(2, rows), stage],
        flops=2 * one_tap,
    )
    return call(
        last_kernel,
        [flags, prior, prior_pair, prior_cross, gain1, weight1, gain2, weight2, bias2, first,
         following, late, inner, near_e, far_e, odd_e],
        [like((frames // 2, rows // 2, half, wide))],
        [window(2, 3), stage, strided, VMEM((2,) + total, F32)],
        flops=one_tap + 3 * one_code,
    )[0]


def solution(mesh):
    placed = (P("group", "row", None, None), P("group"), P("group"), P(), P(), P(), P(), P(), P())
    return jax.shard_map(
        per_device,
        mesh=mesh,
        in_specs=placed,
        out_specs=P("group", "row", None, None),
        check_vma=False,
    )
```

```python
import functools

import jax
import jax.numpy as jnp
from jax import lax
from jax.experimental import pallas as pl
from jax.experimental.pallas import tpu as pltpu
from jax.sharding import PartitionSpec as P

ABOVE = 2
EVEN, TOP, FULL, DISTANCE, BOTTOM, EVEN_GROUP = range(6)
PACK = 30_000_000_000
WHILE_SWAPPED = 4_000_000_000
WHILE_SENT = 2_000_000_000
VMEM = pltpu.VMEM
F32 = jnp.float32
BF16 = jnp.bfloat16


def rotated(value, axis, steps):
    count = lax.axis_size(axis)
    return lax.ppermute(value, axis, [(source, (source + steps) % count) for source in range(count)])


def relayed(value):
    groups, rows = lax.axis_size("group"), lax.axis_size("row")
    pairs = []
    for group in range(groups):
        for row in range(rows):
            if group < 2:
                target = (group, row ^ 1)
            else:
                target = (group + 2 if group + 2 < groups else group + 4 - groups, row)
            pairs.append((group * rows + row, target[0] * rows + target[1]))
    return lax.ppermute(value, ("group", "row"), pairs)


def swapped(value, axis):
    return lax.ppermute(value, axis, [(place, place ^ 1) for place in range(lax.axis_size(axis))])


def crossed_late(value):
    groups, rows = lax.axis_size("group"), lax.axis_size("row")
    planes = groups // 2
    pairs = []
    for group in range(groups):
        plane = group // 2
        for row in range(rows):
            if 0 < row < rows - 1:
                target = (group, ((row + 1) ^ 1) - 1)
            elif 0 < plane < planes - 1 and planes % 2 == 0:
                target = (2 * (((plane + 1) ^ 1) - 1) + group % 2, row)
            else:
                target = (group, rows - 1 - row)
            pairs.append((group * rows + row, target[0] * rows + target[1]))
    return lax.ppermute(value, ("group", "row"), pairs)


def crossed(value):
    groups, rows = lax.axis_size("group"), lax.axis_size("row")
    pairs = []
    for group in range(groups):
        for row in range(rows):
            outer = row in (0, rows - 1)
            target = (group ^ 1, row) if outer else (group, ((row + 1) ^ 1) - 1)
            pairs.append((group * rows + row, target[0] * rows + target[1]))
    return lax.ppermute(value, ("group", "row"), pairs)


def after(first, *values):
    return lax.optimization_barrier((first,) + values)[1:]


def pixel_silu(values, gain):
    inverse = lax.rsqrt(jnp.mean(values * values, axis=-1, keepdims=True) + 1e-06)
    half = values * inverse * (0.5 * gain)
    return half + half * jnp.tanh(half)


def column_window(row):
    width = row.shape[0]
    column = lax.broadcasted_iota(jnp.int32, row.shape, 0)
    left = jnp.where(column == 0, 0.0, pltpu.roll(row, 1, 0))
    right = jnp.where(column == width - 1, 0.0, pltpu.roll(row, width - 1, 0))
    return jnp.concatenate([left.astype(BF16), row.astype(BF16), right.astype(BF16)], axis=-1)


def holds(flag_ref, index):
    return flag_ref[index : index + 1] != 0


def fill_hidden(read, gain, window_ref, frame, rows):
    for row in rows:
        window_ref[frame, row] = column_window(pixel_silu(read(row), gain))


def conv1_rows(window_ref, frame, rows, weight):
    width, depth = window_ref.shape[2], window_ref.shape[3]
    window = jnp.concatenate(
        [window_ref[frame, tap : tap + rows].reshape(rows * width, depth) for tap in range(3)],
        axis=-1,
    )
    return jnp.dot(window, weight.reshape(3 * depth, weight.shape[2]), preferred_element_type=F32)


def fill_second(values, gain, first_row, stage_ref, strided_ref, slot, rows):
    half = strided_ref.shape[2]
    width, channels = 2 * half, stage_ref.shape[2]
    for row in rows:
        ready = pixel_silu(values(row), gain).astype(BF16).astype(F32)
        if row == 0:
            ready = jnp.where(first_row, 0.0, ready)
        stage_ref[row, 0:8] = jnp.zeros((8, channels), F32)
        stage_ref[row, 8 : 8 + width] = ready
        strided_ref[slot, row] = jnp.concatenate(
            [stage_ref[row, pl.ds(7 + tap, half, stride=2), :].astype(BF16) for tap in range(3)],
            axis=-1,
        )


def conv2_frame(weight_ref, *parts):
    windows, weights = [], []
    for strided_ref, slot, step in parts:
        for tap in range(3):
            windows.append(
                jnp.concatenate([strided_ref[slot, tap], strided_ref[slot, tap + 2]], axis=0)
            )
            weights.append(weight_ref[step, tap])
    return jnp.dot(
        jnp.concatenate(windows, axis=-1), jnp.concatenate(weights, axis=0), preferred_element_type=F32
    )


def row_reader(flag_ref, video_ref, frame, pair_ref, cross_ref):
    even, top, bottom = holds(flag_ref, EVEN), holds(flag_ref, TOP), holds(flag_ref, BOTTOM)
    rows = video_ref.shape[1]

    def read(row):
        if ABOVE <= row < ABOVE + rows:
            return video_ref[frame, row - ABOVE].astype(F32)
        if row < ABOVE:
            first, second, outside = cross_ref[frame, row], pair_ref[frame, row], top
        else:
            first, second, outside = pair_ref[frame, 0], cross_ref[frame, 0], bottom
        value = jnp.where(even, first.astype(F32), second.astype(F32))
        return jnp.where(outside, 0.0, value)

    return read


def pack_kernel(flag_ref, video_ref, own_ref, pair_ref, cross_ref):
    even = holds(flag_ref, EVEN)
    frames, rows = video_ref.shape[:2]
    own_ref[...] = video_ref[frames - 2 :]
    split_edges(even, video_ref, frames, rows, pair_ref, cross_ref)


def split_edges(even, source_ref, frames, rows, pair_ref, cross_ref):
    for frame in range(frames):
        for row in range(ABOVE):
            high, low = source_ref[frame, row], source_ref[frame, rows - ABOVE + row]
            pair_ref[frame, row] = jnp.where(even, low, high)
            cross_ref[frame, row] = jnp.where(even, high, low)


def beside(weight_ref, *steps):
    return jnp.concatenate([weight_ref[step] for step in steps], axis=-1)


def send_kernel(
    flag_ref, video_ref, pair_ref, cross_ref, gain1_ref, weight1_ref, bias1_ref,
    gain2_ref, weight2_ref, tail_ref, strided_out_ref, window_ref, stage_ref, total_ref,
):
    first_row = holds(flag_ref, TOP)
    channels = video_ref.shape[3]
    readers = [row_reader(flag_ref, video_ref, f, pair_ref, cross_ref) for f in range(4)]
    for slot, frame in enumerate((1, 2, 3)):
        fill_hidden(readers[frame], gain1_ref[...], window_ref, slot, range(7))
    total_ref[...] = sum(
        conv1_rows(window_ref, step, 5, weight1_ref[step]) for step in range(3)
    ).reshape(total_ref.shape)
    fill_second(
        lambda row: total_ref[row] + readers[3](row + 1) + bias1_ref[...],
        gain2_ref[...], first_row, stage_ref, strided_out_ref, 0, range(5),
    )
    tail = conv2_frame(weight2_ref, (strided_out_ref, 0, 0)).astype(BF16)
    half = strided_out_ref.shape[2]
    for row in range(tail_ref.shape[0]):
        for part in range(2):
            tail_ref[row, part * half : (part + 1) * half] = tail[
                row * half : (row + 1) * half, part * channels : (part + 1) * channels
            ]


def second_kernel(
    flag_ref, video_ref, pair_ref, cross_ref, gain1_ref, weight1_ref, bias1_ref,
    gain2_ref, weight2_ref, bias2_ref, strided3_ref, later_ref, late_ref, window_ref,
    stage_ref, strided_ref, total_ref,
):
    first_row = holds(flag_ref, TOP)
    readers = [row_reader(flag_ref, video_ref, f, pair_ref, cross_ref) for f in range(4)]
    fill_hidden(readers[0], gain1_ref[...], window_ref, 0, range(7))
    total_ref[...] = (
        conv1_rows(window_ref, 0, 5, weight1_ref[0])
        + conv1_rows(later_ref, 0, 5, weight1_ref[1])
        + conv1_rows(later_ref, 1, 5, weight1_ref[2])
    ).reshape(total_ref.shape)
    fill_second(
        lambda row: total_ref[row] + readers[2](row + 1) + bias1_ref[...],
        gain2_ref[...], first_row, stage_ref, strided_ref, 0, range(5),
    )
    late_ref[...] = (
        conv2_frame(weight2_ref, (strided_ref, 0, 1), (strided3_ref, 0, 2)) + bias2_ref[...]
    )


def own_kernel(
    flag_ref, video_ref, pair_ref, cross_ref, weight1_ref, bias1_ref, window_ref, later_ref,
    first_ref, next_ref,
):
    channels = video_ref.shape[3]
    readers = [row_reader(flag_ref, video_ref, f, pair_ref, cross_ref) for f in range(2)]
    both = conv1_rows(window_ref, 0, 5, beside(weight1_ref, 2, 1))
    first_ref[...] = both[:, :channels].reshape(first_ref.shape)
    next_ref[...] = (
        both[:, channels:] + conv1_rows(later_ref, 0, 5, weight1_ref[2])
    ).reshape(next_ref.shape)
    for row in range(5):
        next_ref[row] += readers[1](row + 1) + bias1_ref[...]
        first_ref[row] += readers[0](row + 1) + bias1_ref[...]


def chosen(distance, two, four, odd):
    value = jnp.where(distance == 2, two, odd)
    value = jnp.where(distance == 4, four, value)
    return jnp.where(distance == 0, 0.0, value)


def partner_kernel(start, flag_ref, wanted_ref, own_ref, near_ref, far_ref, out_ref):
    first, one = holds(flag_ref, EVEN_GROUP), wanted_ref[0:1] == 1
    for row in range(out_ref.shape[0]):
        own, near, far = own_ref[start + row], near_ref[start + row], far_ref[row]
        out_ref[row] = jnp.where(
            first, jnp.where(one, own, near), jnp.where(one, near, far)
        )


def prior_kernel(
    flag_ref, two_ref, four0_ref, four1_ref, odd0_ref, odd1_ref, prior_ref, pair_ref, cross_ref,
):
    even, distance = holds(flag_ref, EVEN), flag_ref[DISTANCE : DISTANCE + 1]
    frames, rows = prior_ref.shape[:2]
    for frame, (four_ref, odd_ref) in enumerate(((four0_ref, odd0_ref), (four1_ref, odd1_ref))):
        for row in range(rows):
            prior_ref[frame, row] = chosen(
                distance, two_ref[frame * rows + row], four_ref[row], odd_ref[row]
            )
    split_edges(even, prior_ref, frames, rows, pair_ref, cross_ref)


def inner_kernel(
    flag_ref, prior_ref, gain1_ref, weight1_ref, gain2_ref, first_ref, next_ref,
    first_out_ref, next_out_ref, strided_out_ref, window_ref, stage_ref,
):
    del flag_ref
    rows, width, channels = prior_ref.shape[1:]
    for frame in range(2):
        fill_hidden(
            lambda row: prior_ref[frame, row].astype(F32), gain1_ref[...], window_ref, frame, range(rows)
        )
    first_out_ref[...] = first_ref[...]
    next_out_ref[...] = next_ref[...]
    for tap in range(3):
        low = max(0, ABOVE - tap)
        count = min(rows + 1, rows + ABOVE - tap) - low
        start = low + tap - ABOVE
        shape = (count, width, channels)

        def part(frame, weight):
            window = window_ref[frame, start : start + count]
            return jnp.dot(
                window.reshape(count * width, window.shape[2]), weight, preferred_element_type=F32
            )

        both = part(1, beside(weight1_ref.at[:, tap], 0, 1))
        next_out_ref[low : low + count] += both[:, :channels].reshape(shape)
        first_out_ref[low : low + count] += (
            both[:, channels:] + part(0, weight1_ref[0, tap])
        ).reshape(shape)
    for slot, total_ref in enumerate((next_out_ref, first_out_ref)):
        fill_second(
            lambda row: total_ref[row],
            gain2_ref[...], None, stage_ref, strided_out_ref, slot, range(ABOVE, rows),
        )


def side_by_side(window_ref, frame, taps, weight):
    return jnp.dot(
        jnp.concatenate([window_ref[frame, slot] for slot, _ in taps], axis=-1),
        jnp.concatenate([weight[tap] for _, tap in taps], axis=0),
        preferred_element_type=F32,
    )


def last_kernel(
    flag_ref, prior_ref, pair_ref, cross_ref, gain1_ref, weight1_ref, gain2_ref,
    weight2_ref, bias2_ref, first_ref, next_ref, late_ref, inner_ref, two_ref, four_ref, odd_ref, out_ref,
    window_ref, stage_ref, strided_ref, total_ref,
):
    first_row, keep, distance = holds(flag_ref, TOP), holds(flag_ref, FULL), flag_ref[DISTANCE : DISTANCE + 1]
    rows, width, channels = prior_ref.shape[1:]
    outer = (0, 1, rows + ABOVE)
    for frame in range(2):
        reader = row_reader(flag_ref, prior_ref, frame, pair_ref, cross_ref)
        fill_hidden(
            lambda slot: reader(outer[slot]), gain1_ref[...], window_ref, frame, range(len(outer))
        )
    for target in (0, 1, rows):
        taps = [(slot, place - target) for slot, place in enumerate(outer) if 0 <= place - target < 3]
        total_ref[0, target] = next_ref[target]
        total_ref[1, target] = first_ref[target]
        both = side_by_side(window_ref, 1, taps, beside(weight1_ref, 0, 1))
        total_ref[0, target] += both[:, :channels]
        total_ref[1, target] += both[:, channels:] + side_by_side(
            window_ref, 0, taps, weight1_ref[0]
        )
    for slot in range(2):
        strided_ref[slot, ABOVE:rows] = inner_ref[slot, ABOVE:rows]
        fill_second(
            lambda row: total_ref[slot, row],
            gain2_ref[...], first_row, stage_ref, strided_ref, slot, (0, 1, rows),
        )
    shape = out_ref.shape[1:]
    half = strided_ref.shape[2]
    late = late_ref[...] + conv2_frame(weight2_ref, (strided_ref, 0, 0))
    out_ref[1] = jnp.where(jnp.concatenate([keep, keep], axis=-1), late, 0.0).astype(BF16).reshape(shape)
    early = conv2_frame(weight2_ref, (strided_ref, 0, 2), (strided_ref, 1, 1))
    for row in range(shape[0]):
        tail = chosen(
            distance, two_ref[row].astype(F32), four_ref[row].astype(F32), odd_ref[row].astype(F32)
        )
        tail = jnp.concatenate([tail[:half], tail[half:]], axis=-1)
        part = early[row * half : (row + 1) * half] + bias2_ref[...]
        out_ref[0, row] = (part + tail).astype(BF16)


def call(kernel, operands, outs, scratch, flops=0):
    moved = sum(o.size * o.dtype.itemsize for o in list(operands) + list(outs))
    return pl.pallas_call(
        kernel,
        out_shape=outs,
        in_specs=[pl.BlockSpec(memory_space=VMEM)] * len(operands),
        out_specs=[pl.BlockSpec(memory_space=VMEM)] * len(outs),
        scratch_shapes=scratch,
        compiler_params=pltpu.CompilerParams(vmem_limit_bytes=14 * 1024 * 1024),
        cost_estimate=pl.CostEstimate(flops=flops, bytes_accessed=moved, transcendentals=0),
    )(*operands)


def per_device(
    video_frames, pred_owner, frame_counts, norm1_gain, conv1_weight, conv1_bias, norm2_gain,
    conv2_weight, conv2_bias,
):
    frames, rows, width, channels = video_frames.shape
    wide = conv2_weight.shape[-1]
    half = width // 2
    position = lax.axis_index("group")
    band = lax.axis_index("row")
    distance = jnp.where(pred_owner[0] >= 0, position - pred_owner[0], 0)
    marks = [
        band % 2 == 0, band == 0, frame_counts[0] >= frames, distance,
        band == lax.axis_size("row") - 1, position % 2 == 0,
    ]
    marks += [0] * (8 - len(marks))
    flags = jnp.stack([jnp.full((channels,), mark, F32) for mark in marks])

    def like(value, dtype=BF16):
        return jax.ShapeDtypeStruct(value, dtype)

    def window(count, high):
        return VMEM((count, high, width, 3 * channels), BF16)

    def for_partner(own, near, far, start=0):
        kernel = functools.partial(partner_kernel, start)
        return call(kernel, [flags, wanted, own, near, far], [like(far.shape)], [])[0]

    weight1 = conv1_weight.reshape(3, 3, 3 * channels, channels)
    weight2 = conv2_weight.reshape(3, 3, 3 * channels, wide)
    gain1, bias1 = norm1_gain[None], conv1_bias[None]
    gain2, bias2 = norm2_gain[None], conv2_bias[None]
    pair_of = like((2, rows, width, channels))
    flat = (2 * rows, width, channels)
    total = (rows + 1, width, channels)
    stage = VMEM((rows + 1, width + 16, channels), F32)
    strided = VMEM((2, rows + 1, half, 3 * channels), BF16)
    one_tap = 2 * (rows + 1) * width * 9 * channels * channels
    one_code = 2 * (rows // 2) * half * 9 * channels * wide

    edge = like((frames, ABOVE, width, channels))
    own, pair, cross = call(
        pack_kernel, [flags, video_frames], [pair_of, edge, edge], [], flops=PACK
    )
    wanted = swapped(jnp.full((8, channels), distance, F32), "group")
    cross = crossed(after(wanted, cross)[0])
    own = own.reshape(flat)
    near = rotated(own, "group", 2)
    pair = swapped(pair, "row")
    fars = [
        relayed(lax.slice_in_dim(near, frame * rows, (frame + 1) * rows, axis=0))
        for frame in range(2)
    ]
    pair, cross = after(near, pair, cross)
    def windows(count):
        return like((count, rows + 3, width, 3 * channels))

    own_e, strided3, later = call(
        send_kernel,
        [flags, video_frames, pair, cross, gain1, weight1, bias1, gain2, weight2],
        [
            like((rows // 2, width, channels)), like((1, rows + 1, half, 3 * channels)),
            windows(3),
        ],
        [stage, VMEM(total, F32)],
        flops=3 * one_tap + one_code,
    )
    chosen_first = for_partner(own, near, after(own_e, fars[0])[0])
    chosen_own = for_partner(own, near, after(chosen_first, fars[1])[0], rows)
    odds = [swapped(chosen_first, "group"), swapped(chosen_own, "group")]
    near_e = rotated(own_e, "group", 2)
    late, start = call(
        second_kernel,
        [
            flags, video_frames, pair, cross, gain1, weight1, bias1, gain2, weight2, bias2,
            after(chosen_own, strided3)[0], later,
        ],
        [like((rows // 2 * half, wide), F32), windows(1)],
        [stage, strided, VMEM(total, F32)],
        flops=WHILE_SWAPPED,
    )
    near_e = after(late, near_e)[0]
    far_e = relayed(near_e)
    first, following = call(
        own_kernel,
        [flags, video_frames, pair, cross, weight1, bias1, after(near_e, start)[0], later],
        [like(total, F32), like(total, F32)],
        [],
        flops=WHILE_SENT,
    )
    odd_e = swapped(for_partner(own_e, near_e, far_e), "group")
    edge = like((2, ABOVE, width, channels))
    prior, prior_pair, prior_cross = call(
        prior_kernel, [flags, near] + fars + [odds[0], after(first, odds[1])[0]], [pair_of, edge, edge], []
    )
    prior_cross = crossed_late(prior_cross)
    prior_pair = swapped(prior_pair, "row")
    first, following, inner = call(
        inner_kernel,
        [flags, prior, gain1, weight1, gain2, first, following],
        [like(total, F32), like(total, F32), like((2, rows + 1, half, 3 * channels))],
        [window(2, rows), stage],
        flops=2 * one_tap,
    )
    return call(
        last_kernel,
        [flags, prior, prior_pair, prior_cross, gain1, weight1, gain2, weight2, bias2, first,
         following, late, inner, near_e, far_e, odd_e],
        [like((frames // 2, rows // 2, half, wide))],
        [window(2, 3), stage, strided, VMEM((2,) + total, F32)],
        flops=one_tap + 3 * one_code,
    )[0]


def solution(mesh):
    placed = (P("group", "row", None, None), P("group"), P("group"), P(), P(), P(), P(), P(), P())
    return jax.shard_map(
        per_device,
        mesh=mesh,
        in_specs=placed,
        out_specs=P("group", "row", None, None),
        check_vma=False,
    )
```

```python
import functools

import jax
import jax.numpy as jnp
from jax import lax
from jax.experimental import pallas as pl
from jax.experimental.pallas import tpu as pltpu
from jax.sharding import PartitionSpec as P

ABOVE = 2
EVEN, TOP, FULL, DISTANCE, BOTTOM, EVEN_GROUP = range(6)
PACK = 30_000_000_000
WHILE_SWAPPED = 3_000_000_000
WHILE_SENT = 200_000_000
VMEM = pltpu.VMEM
F32 = jnp.float32
BF16 = jnp.bfloat16


def rotated(value, axis, steps):
    count = lax.axis_size(axis)
    return lax.ppermute(value, axis, [(source, (source + steps) % count) for source in range(count)])


def relayed(value):
    groups, rows = lax.axis_size("group"), lax.axis_size("row")
    pairs = []
    for group in range(groups):
        for row in range(rows):
            if group < 2:
                target = (group, row ^ 1)
            else:
                target = (group + 2 if group + 2 < groups else group + 4 - groups, row)
            pairs.append((group * rows + row, target[0] * rows + target[1]))
    return lax.ppermute(value, ("group", "row"), pairs)


def swapped(value, axis):
    return lax.ppermute(value, axis, [(place, place ^ 1) for place in range(lax.axis_size(axis))])


def crossed_late(value):
    groups, rows = lax.axis_size("group"), lax.axis_size("row")
    planes = groups // 2
    pairs = []
    for group in range(groups):
        plane = group // 2
        for row in range(rows):
            if 0 < row < rows - 1:
                target = (group, ((row + 1) ^ 1) - 1)
            elif 0 < plane < planes - 1 and planes % 2 == 0:
                target = (2 * (((plane + 1) ^ 1) - 1) + group % 2, row)
            else:
                target = (group, rows - 1 - row)
            pairs.append((group * rows + row, target[0] * rows + target[1]))
    return lax.ppermute(value, ("group", "row"), pairs)


def crossed(value):
    groups, rows = lax.axis_size("group"), lax.axis_size("row")
    pairs = []
    for group in range(groups):
        for row in range(rows):
            outer = row in (0, rows - 1)
            target = (group ^ 1, row) if outer else (group, ((row + 1) ^ 1) - 1)
            pairs.append((group * rows + row, target[0] * rows + target[1]))
    return lax.ppermute(value, ("group", "row"), pairs)


def after(first, *values):
    return lax.optimization_barrier((first,) + values)[1:]


def pixel_silu(values, gain):
    inverse = lax.rsqrt(jnp.mean(values * values, axis=-1, keepdims=True) + 1e-06)
    half = values * inverse * (0.5 * gain)
    return half + half * jnp.tanh(half)


def column_window(row):
    width = row.shape[0]
    column = lax.broadcasted_iota(jnp.int32, row.shape, 0)
    left = jnp.where(column == 0, 0.0, pltpu.roll(row, 1, 0))
    right = jnp.where(column == width - 1, 0.0, pltpu.roll(row, width - 1, 0))
    return jnp.concatenate([left.astype(BF16), row.astype(BF16), right.astype(BF16)], axis=-1)


def holds(flag_ref, index):
    return flag_ref[index : index + 1] != 0


def fill_hidden(read, gain, window_ref, frame, rows):
    for row in rows:
        window_ref[frame, row] = column_window(pixel_silu(read(row), gain))


def conv1_rows(window_ref, frame, rows, weight):
    width, depth = window_ref.shape[2], window_ref.shape[3]
    window = jnp.concatenate(
        [window_ref[frame, tap : tap + rows].reshape(rows * width, depth) for tap in range(3)],
        axis=-1,
    )
    return jnp.dot(window, weight.reshape(3 * depth, weight.shape[2]), preferred_element_type=F32)


def fill_second(values, gain, first_row, stage_ref, strided_ref, slot, rows):
    half = strided_ref.shape[2]
    width, channels = 2 * half, stage_ref.shape[2]
    for row in rows:
        ready = pixel_silu(values(row), gain).astype(BF16).astype(F32)
        if row == 0:
            ready = jnp.where(first_row, 0.0, ready)
        stage_ref[row, 0:8] = jnp.zeros((8, channels), F32)
        stage_ref[row, 8 : 8 + width] = ready
        strided_ref[slot, row] = jnp.concatenate(
            [stage_ref[row, pl.ds(7 + tap, half, stride=2), :].astype(BF16) for tap in range(3)],
            axis=-1,
        )


def conv2_frame(weight_ref, *parts):
    windows, weights = [], []
    for strided_ref, slot, step in parts:
        for tap in range(3):
            windows.append(
                jnp.concatenate([strided_ref[slot, tap], strided_ref[slot, tap + 2]], axis=0)
            )
            weights.append(weight_ref[step, tap])
    return jnp.dot(
        jnp.concatenate(windows, axis=-1), jnp.concatenate(weights, axis=0), preferred_element_type=F32
    )


def row_reader(flag_ref, video_ref, frame, pair_ref, cross_ref):
    even, top, bottom = holds(flag_ref, EVEN), holds(flag_ref, TOP), holds(flag_ref, BOTTOM)
    rows = video_ref.shape[1]

    def read(row):
        if ABOVE <= row < ABOVE + rows:
            return video_ref[frame, row - ABOVE].astype(F32)
        if row < ABOVE:
            first, second, outside = cross_ref[frame, row], pair_ref[frame, row], top
        else:
            first, second, outside = pair_ref[frame, 0], cross_ref[frame, 0], bottom
        value = jnp.where(even, first.astype(F32), second.astype(F32))
        return jnp.where(outside, 0.0, value)

    return read


def pack_kernel(flag_ref, video_ref, own_ref, pair_ref, cross_ref):
    even = holds(flag_ref, EVEN)
    frames, rows = video_ref.shape[:2]
    own_ref[...] = video_ref[frames - 2 :]
    split_edges(even, video_ref, frames, rows, pair_ref, cross_ref)


def split_edges(even, source_ref, frames, rows, pair_ref, cross_ref):
    for frame in range(frames):
        for row in range(ABOVE):
            high, low = source_ref[frame, row], source_ref[frame, rows - ABOVE + row]
            pair_ref[frame, row] = jnp.where(even, low, high)
            cross_ref[frame, row] = jnp.where(even, high, low)


def beside(weight_ref, *steps):
    return jnp.concatenate([weight_ref[step] for step in steps], axis=-1)


def send_kernel(
    flag_ref, video_ref, pair_ref, cross_ref, gain1_ref, weight1_ref, bias1_ref,
    gain2_ref, weight2_ref, tail_ref, strided_out_ref, window_ref, stage_ref, total_ref,
):
    first_row = holds(flag_ref, TOP)
    channels = video_ref.shape[3]
    readers = [row_reader(flag_ref, video_ref, f, pair_ref, cross_ref) for f in range(4)]
    for slot, frame in enumerate((1, 2, 3)):
        fill_hidden(readers[frame], gain1_ref[...], window_ref, slot, range(7))
    total_ref[...] = sum(
        conv1_rows(window_ref, step, 5, weight1_ref[step]) for step in range(3)
    ).reshape(total_ref.shape)
    fill_second(
        lambda row: total_ref[row] + readers[3](row + 1) + bias1_ref[...],
        gain2_ref[...], first_row, stage_ref, strided_out_ref, 0, range(5),
    )
    tail = conv2_frame(weight2_ref, (strided_out_ref, 0, 0)).astype(BF16)
    half = strided_out_ref.shape[2]
    for row in range(tail_ref.shape[0]):
        for part in range(2):
            tail_ref[row, part * half : (part + 1) * half] = tail[
                row * half : (row + 1) * half, part * channels : (part + 1) * channels
            ]


def second_kernel(
    flag_ref, video_ref, pair_ref, cross_ref, gain1_ref, weight1_ref, bias1_ref,
    gain2_ref, weight2_ref, bias2_ref, strided3_ref, later_ref, late_ref, window_ref,
    stage_ref, strided_ref, total_ref,
):
    first_row = holds(flag_ref, TOP)
    readers = [row_reader(flag_ref, video_ref, f, pair_ref, cross_ref) for f in range(4)]
    fill_hidden(readers[0], gain1_ref[...], window_ref, 0, range(7))
    total_ref[...] = (
        conv1_rows(window_ref, 0, 5, weight1_ref[0])
        + conv1_rows(later_ref, 0, 5, weight1_ref[1])
        + conv1_rows(later_ref, 1, 5, weight1_ref[2])
    ).reshape(total_ref.shape)
    fill_second(
        lambda row: total_ref[row] + readers[2](row + 1) + bias1_ref[...],
        gain2_ref[...], first_row, stage_ref, strided_ref, 0, range(5),
    )
    late_ref[...] = (
        conv2_frame(weight2_ref, (strided_ref, 0, 1), (strided3_ref, 0, 2)) + bias2_ref[...]
    )


def own_kernel(
    flag_ref, video_ref, pair_ref, cross_ref, weight1_ref, bias1_ref, window_ref, later_ref,
    first_ref, next_ref,
):
    channels = video_ref.shape[3]
    readers = [row_reader(flag_ref, video_ref, f, pair_ref, cross_ref) for f in range(2)]
    both = conv1_rows(window_ref, 0, 5, beside(weight1_ref, 2, 1))
    first_ref[...] = both[:, :channels].reshape(first_ref.shape)
    next_ref[...] = (
        both[:, channels:] + conv1_rows(later_ref, 0, 5, weight1_ref[2])
    ).reshape(next_ref.shape)
    for row in range(5):
        next_ref[row] += readers[1](row + 1) + bias1_ref[...]
        first_ref[row] += readers[0](row + 1) + bias1_ref[...]


def chosen(distance, two, four, odd):
    value = jnp.where(distance == 2, two, odd)
    value = jnp.where(distance == 4, four, value)
    return jnp.where(distance == 0, 0.0, value)


def partner_kernel(start, flag_ref, wanted_ref, own_ref, near_ref, far_ref, out_ref):
    first, one = holds(flag_ref, EVEN_GROUP), wanted_ref[0:1] == 1
    for row in range(out_ref.shape[0]):
        own, near, far = own_ref[start + row], near_ref[start + row], far_ref[row]
        out_ref[row] = jnp.where(
            first, jnp.where(one, own, near), jnp.where(one, near, far)
        )


def prior_kernel(
    flag_ref, two_ref, four0_ref, four1_ref, odd0_ref, odd1_ref, prior_ref, pair_ref, cross_ref,
):
    even, distance = holds(flag_ref, EVEN), flag_ref[DISTANCE : DISTANCE + 1]
    frames, rows = prior_ref.shape[:2]
    for frame, (four_ref, odd_ref) in enumerate(((four0_ref, odd0_ref), (four1_ref, odd1_ref))):
        for row in range(rows):
            prior_ref[frame, row] = chosen(
                distance, two_ref[frame * rows + row], four_ref[row], odd_ref[row]
            )
    split_edges(even, prior_ref, frames, rows, pair_ref, cross_ref)


def inner_kernel(
    flag_ref, prior_ref, gain1_ref, weight1_ref, gain2_ref, first_ref, next_ref,
    first_out_ref, next_out_ref, strided_out_ref, window_ref, stage_ref,
):
    del flag_ref
    rows, width, channels = prior_ref.shape[1:]
    for frame in range(2):
        fill_hidden(
            lambda row: prior_ref[frame, row].astype(F32), gain1_ref[...], window_ref, frame, range(rows)
        )
    first_out_ref[...] = first_ref[...]
    next_out_ref[...] = next_ref[...]
    for tap in range(3):
        low = max(0, ABOVE - tap)
        count = min(rows + 1, rows + ABOVE - tap) - low
        start = low + tap - ABOVE
        shape = (count, width, channels)

        def part(frame, weight):
            window = window_ref[frame, start : start + count]
            return jnp.dot(
                window.reshape(count * width, window.shape[2]), weight, preferred_element_type=F32
            )

        both = part(1, beside(weight1_ref.at[:, tap], 0, 1))
        next_out_ref[low : low + count] += both[:, :channels].reshape(shape)
        first_out_ref[low : low + count] += (
            both[:, channels:] + part(0, weight1_ref[0, tap])
        ).reshape(shape)
    for slot, total_ref in enumerate((next_out_ref, first_out_ref)):
        fill_second(
            lambda row: total_ref[row],
            gain2_ref[...], None, stage_ref, strided_out_ref, slot, range(ABOVE, rows),
        )


def side_by_side(window_ref, frame, taps, weight):
    return jnp.dot(
        jnp.concatenate([window_ref[frame, slot] for slot, _ in taps], axis=-1),
        jnp.concatenate([weight[tap] for _, tap in taps], axis=0),
        preferred_element_type=F32,
    )


def last_kernel(
    flag_ref, prior_ref, pair_ref, cross_ref, gain1_ref, weight1_ref, gain2_ref,
    weight2_ref, bias2_ref, first_ref, next_ref, late_ref, inner_ref, two_ref, four_ref, odd_ref, out_ref,
    window_ref, stage_ref, strided_ref, total_ref,
):
    first_row, keep, distance = holds(flag_ref, TOP), holds(flag_ref, FULL), flag_ref[DISTANCE : DISTANCE + 1]
    rows, width, channels = prior_ref.shape[1:]
    outer = (0, 1, rows + ABOVE)
    for frame in range(2):
        reader = row_reader(flag_ref, prior_ref, frame, pair_ref, cross_ref)
        fill_hidden(
            lambda slot: reader(outer[slot]), gain1_ref[...], window_ref, frame, range(len(outer))
        )
    for target in (0, 1, rows):
        taps = [(slot, place - target) for slot, place in enumerate(outer) if 0 <= place - target < 3]
        total_ref[0, target] = next_ref[target]
        total_ref[1, target] = first_ref[target]
        both = side_by_side(window_ref, 1, taps, beside(weight1_ref, 0, 1))
        total_ref[0, target] += both[:, :channels]
        total_ref[1, target] += both[:, channels:] + side_by_side(
            window_ref, 0, taps, weight1_ref[0]
        )
    for slot in range(2):
        strided_ref[slot, ABOVE:rows] = inner_ref[slot, ABOVE:rows]
        fill_second(
            lambda row: total_ref[slot, row],
            gain2_ref[...], first_row, stage_ref, strided_ref, slot, (0, 1, rows),
        )
    shape = out_ref.shape[1:]
    half = strided_ref.shape[2]
    late = late_ref[...] + conv2_frame(weight2_ref, (strided_ref, 0, 0))
    out_ref[1] = jnp.where(jnp.concatenate([keep, keep], axis=-1), late, 0.0).astype(BF16).reshape(shape)
    early = conv2_frame(weight2_ref, (strided_ref, 0, 2), (strided_ref, 1, 1))
    for row in range(shape[0]):
        tail = chosen(
            distance, two_ref[row].astype(F32), four_ref[row].astype(F32), odd_ref[row].astype(F32)
        )
        tail = jnp.concatenate([tail[:half], tail[half:]], axis=-1)
        part = early[row * half : (row + 1) * half] + bias2_ref[...]
        out_ref[0, row] = (part + tail).astype(BF16)


def call(kernel, operands, outs, scratch, flops=0):
    moved = sum(o.size * o.dtype.itemsize for o in list(operands) + list(outs))
    return pl.pallas_call(
        kernel,
        out_shape=outs,
        in_specs=[pl.BlockSpec(memory_space=VMEM)] * len(operands),
        out_specs=[pl.BlockSpec(memory_space=VMEM)] * len(outs),
        scratch_shapes=scratch,
        compiler_params=pltpu.CompilerParams(vmem_limit_bytes=14 * 1024 * 1024),
        cost_estimate=pl.CostEstimate(flops=flops, bytes_accessed=moved, transcendentals=0),
    )(*operands)


def per_device(
    video_frames, pred_owner, frame_counts, norm1_gain, conv1_weight, conv1_bias, norm2_gain,
    conv2_weight, conv2_bias,
):
    frames, rows, width, channels = video_frames.shape
    wide = conv2_weight.shape[-1]
    half = width // 2
    position = lax.axis_index("group")
    band = lax.axis_index("row")
    distance = jnp.where(pred_owner[0] >= 0, position - pred_owner[0], 0)
    marks = [
        band % 2 == 0, band == 0, frame_counts[0] >= frames, distance,
        band == lax.axis_size("row") - 1, position % 2 == 0,
    ]
    marks += [0] * (8 - len(marks))
    flags = jnp.stack([jnp.full((channels,), mark, F32) for mark in marks])

    def like(value, dtype=BF16):
        return jax.ShapeDtypeStruct(value, dtype)

    def window(count, high):
        return VMEM((count, high, width, 3 * channels), BF16)

    def for_partner(own, near, far, start=0):
        kernel = functools.partial(partner_kernel, start)
        return call(kernel, [flags, wanted, own, near, far], [like(far.shape)], [])[0]

    weight1 = conv1_weight.reshape(3, 3, 3 * channels, channels)
    weight2 = conv2_weight.reshape(3, 3, 3 * channels, wide)
    gain1, bias1 = norm1_gain[None], conv1_bias[None]
    gain2, bias2 = norm2_gain[None], conv2_bias[None]
    pair_of = like((2, rows, width, channels))
    flat = (2 * rows, width, channels)
    total = (rows + 1, width, channels)
    stage = VMEM((rows + 1, width + 16, channels), F32)
    strided = VMEM((2, rows + 1, half, 3 * channels), BF16)
    one_tap = 2 * (rows + 1) * width * 9 * channels * channels
    one_code = 2 * (rows // 2) * half * 9 * channels * wide

    edge = like((frames, ABOVE, width, channels))
    own, pair, cross = call(
        pack_kernel, [flags, video_frames], [pair_of, edge, edge], [], flops=PACK
    )
    wanted = swapped(jnp.full((8, channels), distance, F32), "group")
    cross = crossed(after(wanted, cross)[0])
    own = own.reshape(flat)
    near = rotated(own, "group", 2)
    pair = swapped(pair, "row")
    fars = [
        relayed(lax.slice_in_dim(near, frame * rows, (frame + 1) * rows, axis=0))
        for frame in range(2)
    ]
    pair, cross = after(near, pair, cross)
    def windows(count):
        return like((count, rows + 3, width, 3 * channels))

    own_e, strided3, later = call(
        send_kernel,
        [flags, video_frames, pair, cross, gain1, weight1, bias1, gain2, weight2],
        [
            like((rows // 2, width, channels)), like((1, rows + 1, half, 3 * channels)),
            windows(3),
        ],
        [stage, VMEM(total, F32)],
        flops=3 * one_tap + one_code,
    )
    chosen_first = for_partner(own, near, after(own_e, fars[0])[0])
    chosen_own = for_partner(own, near, after(chosen_first, fars[1])[0], rows)
    odds = [swapped(chosen_first, "group"), swapped(chosen_own, "group")]
    near_e = after(chosen_own, rotated(own_e, "group", 2))[0]
    late, start = call(
        second_kernel,
        [
            flags, video_frames, pair, cross, gain1, weight1, bias1, gain2, weight2, bias2,
            after(near_e, strided3)[0], later,
        ],
        [like((rows // 2 * half, wide), F32), windows(1)],
        [stage, strided, VMEM(total, F32)],
        flops=WHILE_SWAPPED,
    )
    far_e = relayed(near_e)
    first, following = call(
        own_kernel,
        [flags, video_frames, pair, cross, weight1, bias1, start, later],
        [like(total, F32), like(total, F32)],
        [],
        flops=WHILE_SENT,
    )
    odd_e = swapped(for_partner(own_e, near_e, far_e), "group")
    edge = like((2, ABOVE, width, channels))
    prior, prior_pair, prior_cross = call(
        prior_kernel, [flags, near] + fars + [odds[0], after(late, odds[1])[0]], [pair_of, edge, edge], []
    )
    prior_cross = crossed_late(prior_cross)
    prior_pair = swapped(prior_pair, "row")
    first, following, inner = call(
        inner_kernel,
        [flags, prior, gain1, weight1, gain2, first, following],
        [like(total, F32), like(total, F32), like((2, rows + 1, half, 3 * channels))],
        [window(2, rows), stage],
        flops=2 * one_tap,
    )
    return call(
        last_kernel,
        [flags, prior, prior_pair, prior_cross, gain1, weight1, gain2, weight2, bias2, first,
         following, late, inner, near_e, far_e, odd_e],
        [like((frames // 2, rows // 2, half, wide))],
        [window(2, 3), stage, strided, VMEM((2,) + total, F32)],
        flops=one_tap + 3 * one_code,
    )[0]


def solution(mesh):
    placed = (P("group", "row", None, None), P("group"), P("group"), P(), P(), P(), P(), P(), P())
    return jax.shard_map(
        per_device,
        mesh=mesh,
        in_specs=placed,
        out_specs=P("group", "row", None, None),
        check_vma=False,
    )
```

```python
import functools

import jax
import jax.numpy as jnp
from jax import lax
from jax.experimental import pallas as pl
from jax.experimental.pallas import tpu as pltpu
from jax.sharding import PartitionSpec as P

ABOVE = 2
EVEN, TOP, FULL, DISTANCE, BOTTOM, EVEN_GROUP = range(6)
PACK = 30_000_000_000
WHILE_SWAPPED = 3_000_000_000
WHILE_SENT = 200_000_000
VMEM = pltpu.VMEM
F32 = jnp.float32
BF16 = jnp.bfloat16


def rotated(value, axis, steps):
    count = lax.axis_size(axis)
    return lax.ppermute(value, axis, [(source, (source + steps) % count) for source in range(count)])


def relayed(value):
    groups, rows = lax.axis_size("group"), lax.axis_size("row")
    pairs = []
    for group in range(groups):
        for row in range(rows):
            if group < 2:
                target = (group, row ^ 1)
            else:
                target = (group + 2 if group + 2 < groups else group + 4 - groups, row)
            pairs.append((group * rows + row, target[0] * rows + target[1]))
    return lax.ppermute(value, ("group", "row"), pairs)


def swapped(value, axis):
    return lax.ppermute(value, axis, [(place, place ^ 1) for place in range(lax.axis_size(axis))])


def crossed_late(value):
    groups, rows = lax.axis_size("group"), lax.axis_size("row")
    planes = groups // 2
    pairs = []
    for group in range(groups):
        plane = group // 2
        for row in range(rows):
            if 0 < row < rows - 1:
                target = (group, ((row + 1) ^ 1) - 1)
            elif 0 < plane < planes - 1 and planes % 2 == 0:
                target = (2 * (((plane + 1) ^ 1) - 1) + group % 2, row)
            else:
                target = (group, rows - 1 - row)
            pairs.append((group * rows + row, target[0] * rows + target[1]))
    return lax.ppermute(value, ("group", "row"), pairs)


def crossed(value):
    groups, rows = lax.axis_size("group"), lax.axis_size("row")
    pairs = []
    for group in range(groups):
        for row in range(rows):
            outer = row in (0, rows - 1)
            target = (group ^ 1, row) if outer else (group, ((row + 1) ^ 1) - 1)
            pairs.append((group * rows + row, target[0] * rows + target[1]))
    return lax.ppermute(value, ("group", "row"), pairs)


def after(first, *values):
    return lax.optimization_barrier((first,) + values)[1:]


def pixel_silu(values, gain):
    inverse = lax.rsqrt(jnp.mean(values * values, axis=-1, keepdims=True) + 1e-06)
    half = values * inverse * (0.5 * gain)
    return half + half * jnp.tanh(half)


def column_window(row):
    width = row.shape[0]
    column = lax.broadcasted_iota(jnp.int32, row.shape, 0)
    left = jnp.where(column == 0, 0.0, pltpu.roll(row, 1, 0))
    right = jnp.where(column == width - 1, 0.0, pltpu.roll(row, width - 1, 0))
    return jnp.concatenate([left.astype(BF16), row.astype(BF16), right.astype(BF16)], axis=-1)


def holds(flag_ref, index):
    return flag_ref[index : index + 1] != 0


def fill_hidden(read, gain, window_ref, frame, rows):
    for row in rows:
        window_ref[frame, row] = column_window(pixel_silu(read(row), gain))


def conv1_rows(window_ref, frame, rows, weight):
    width, depth = window_ref.shape[2], window_ref.shape[3]
    window = jnp.concatenate(
        [window_ref[frame, tap : tap + rows].reshape(rows * width, depth) for tap in range(3)],
        axis=-1,
    )
    return jnp.dot(window, weight.reshape(3 * depth, weight.shape[2]), preferred_element_type=F32)


def fill_second(values, gain, first_row, stage_ref, strided_ref, slot, rows):
    half = strided_ref.shape[2]
    width, channels = 2 * half, stage_ref.shape[2]
    for row in rows:
        ready = pixel_silu(values(row), gain).astype(BF16).astype(F32)
        if row == 0:
            ready = jnp.where(first_row, 0.0, ready)
        stage_ref[row, 0:8] = jnp.zeros((8, channels), F32)
        stage_ref[row, 8 : 8 + width] = ready
        strided_ref[slot, row] = jnp.concatenate(
            [stage_ref[row, pl.ds(7 + tap, half, stride=2), :].astype(BF16) for tap in range(3)],
            axis=-1,
        )


def conv2_frame(weight_ref, *parts):
    windows, weights = [], []
    for strided_ref, slot, step in parts:
        for tap in range(3):
            windows.append(
                jnp.concatenate([strided_ref[slot, tap], strided_ref[slot, tap + 2]], axis=0)
            )
            weights.append(weight_ref[step, tap])
    return jnp.dot(
        jnp.concatenate(windows, axis=-1), jnp.concatenate(weights, axis=0), preferred_element_type=F32
    )


def row_reader(flag_ref, video_ref, frame, pair_ref, cross_ref):
    even, top, bottom = holds(flag_ref, EVEN), holds(flag_ref, TOP), holds(flag_ref, BOTTOM)
    rows = video_ref.shape[1]

    def read(row):
        if ABOVE <= row < ABOVE + rows:
            return video_ref[frame, row - ABOVE].astype(F32)
        if row < ABOVE:
            first, second, outside = cross_ref[frame, row], pair_ref[frame, row], top
        else:
            first, second, outside = pair_ref[frame, 0], cross_ref[frame, 0], bottom
        value = jnp.where(even, first.astype(F32), second.astype(F32))
        return jnp.where(outside, 0.0, value)

    return read


def pack_kernel(flag_ref, video_ref, own_ref, pair_ref, cross_ref):
    even = holds(flag_ref, EVEN)
    frames, rows = video_ref.shape[:2]
    own_ref[...] = video_ref[frames - 2 :]
    split_edges(even, video_ref, frames, rows, pair_ref, cross_ref)


def split_edges(even, source_ref, frames, rows, pair_ref, cross_ref):
    for frame in range(frames):
        for row in range(ABOVE):
            high, low = source_ref[frame, row], source_ref[frame, rows - ABOVE + row]
            pair_ref[frame, row] = jnp.where(even, low, high)
            cross_ref[frame, row] = jnp.where(even, high, low)


def beside(weight_ref, *steps):
    return jnp.concatenate([weight_ref[step] for step in steps], axis=-1)


def send_kernel(
    flag_ref, video_ref, pair_ref, cross_ref, gain1_ref, weight1_ref, bias1_ref,
    gain2_ref, weight2_ref, tail_ref, strided_out_ref, window_ref, stage_ref, total_ref,
):
    first_row = holds(flag_ref, TOP)
    channels = video_ref.shape[3]
    readers = [row_reader(flag_ref, video_ref, f, pair_ref, cross_ref) for f in range(4)]
    for slot, frame in enumerate((1, 2, 3)):
        fill_hidden(readers[frame], gain1_ref[...], window_ref, slot, range(7))
    total_ref[...] = sum(
        conv1_rows(window_ref, step, 5, weight1_ref[step]) for step in range(3)
    ).reshape(total_ref.shape)
    fill_second(
        lambda row: total_ref[row] + readers[3](row + 1) + bias1_ref[...],
        gain2_ref[...], first_row, stage_ref, strided_out_ref, 0, range(5),
    )
    tail = conv2_frame(weight2_ref, (strided_out_ref, 0, 0)).astype(BF16)
    half = strided_out_ref.shape[2]
    for row in range(tail_ref.shape[0]):
        for part in range(2):
            tail_ref[row, part * half : (part + 1) * half] = tail[
                row * half : (row + 1) * half, part * channels : (part + 1) * channels
            ]


def second_kernel(
    flag_ref, video_ref, pair_ref, cross_ref, weight1_ref, bias1_ref,
    gain2_ref, weight2_ref, bias2_ref, strided3_ref, window_ref, later_ref, late_ref,
    stage_ref, strided_ref, total_ref,
):
    first_row = holds(flag_ref, TOP)
    readers = [row_reader(flag_ref, video_ref, f, pair_ref, cross_ref) for f in range(4)]
    total_ref[...] = (
        conv1_rows(window_ref, 0, 5, weight1_ref[0])
        + conv1_rows(later_ref, 0, 5, weight1_ref[1])
        + conv1_rows(later_ref, 1, 5, weight1_ref[2])
    ).reshape(total_ref.shape)
    fill_second(
        lambda row: total_ref[row] + readers[2](row + 1) + bias1_ref[...],
        gain2_ref[...], first_row, stage_ref, strided_ref, 0, range(5),
    )
    late_ref[...] = (
        conv2_frame(weight2_ref, (strided_ref, 0, 1), (strided3_ref, 0, 2)) + bias2_ref[...]
    )


def own_kernel(
    flag_ref, video_ref, pair_ref, cross_ref, gain1_ref, weight1_ref, bias1_ref, later_ref,
    first_ref, next_ref, window_ref,
):
    channels = video_ref.shape[3]
    readers = [row_reader(flag_ref, video_ref, f, pair_ref, cross_ref) for f in range(2)]
    fill_hidden(readers[0], gain1_ref[...], window_ref, 0, range(7))
    both = conv1_rows(window_ref, 0, 5, beside(weight1_ref, 2, 1))
    first_ref[...] = both[:, :channels].reshape(first_ref.shape)
    next_ref[...] = (
        both[:, channels:] + conv1_rows(later_ref, 0, 5, weight1_ref[2])
    ).reshape(next_ref.shape)
    for row in range(5):
        next_ref[row] += readers[1](row + 1) + bias1_ref[...]
        first_ref[row] += readers[0](row + 1) + bias1_ref[...]


def chosen(distance, two, four, odd):
    value = jnp.where(distance == 2, two, odd)
    value = jnp.where(distance == 4, four, value)
    return jnp.where(distance == 0, 0.0, value)


def partner_kernel(start, flag_ref, wanted_ref, own_ref, near_ref, far_ref, out_ref):
    first, one = holds(flag_ref, EVEN_GROUP), wanted_ref[0:1] == 1
    for row in range(out_ref.shape[0]):
        own, near, far = own_ref[start + row], near_ref[start + row], far_ref[row]
        out_ref[row] = jnp.where(
            first, jnp.where(one, own, near), jnp.where(one, near, far)
        )


def prior_kernel(
    flag_ref, two_ref, four0_ref, four1_ref, odd0_ref, odd1_ref, prior_ref, pair_ref, cross_ref,
):
    even, distance = holds(flag_ref, EVEN), flag_ref[DISTANCE : DISTANCE + 1]
    frames, rows = prior_ref.shape[:2]
    for frame, (four_ref, odd_ref) in enumerate(((four0_ref, odd0_ref), (four1_ref, odd1_ref))):
        for row in range(rows):
            prior_ref[frame, row] = chosen(
                distance, two_ref[frame * rows + row], four_ref[row], odd_ref[row]
            )
    split_edges(even, prior_ref, frames, rows, pair_ref, cross_ref)


def inner_kernel(
    flag_ref, prior_ref, gain1_ref, weight1_ref, gain2_ref, first_ref, next_ref,
    first_out_ref, next_out_ref, strided_out_ref, window_ref, stage_ref,
):
    del flag_ref
    rows, width, channels = prior_ref.shape[1:]
    for frame in range(2):
        fill_hidden(
            lambda row: prior_ref[frame, row].astype(F32), gain1_ref[...], window_ref, frame, range(rows)
        )
    first_out_ref[...] = first_ref[...]
    next_out_ref[...] = next_ref[...]
    for tap in range(3):
        low = max(0, ABOVE - tap)
        count = min(rows + 1, rows + ABOVE - tap) - low
        start = low + tap - ABOVE
        shape = (count, width, channels)

        def part(frame, weight):
            window = window_ref[frame, start : start + count]
            return jnp.dot(
                window.reshape(count * width, window.shape[2]), weight, preferred_element_type=F32
            )

        both = part(1, beside(weight1_ref.at[:, tap], 0, 1))
        next_out_ref[low : low + count] += both[:, :channels].reshape(shape)
        first_out_ref[low : low + count] += (
            both[:, channels:] + part(0, weight1_ref[0, tap])
        ).reshape(shape)
    for slot, total_ref in enumerate((next_out_ref, first_out_ref)):
        fill_second(
            lambda row: total_ref[row],
            gain2_ref[...], None, stage_ref, strided_out_ref, slot, range(ABOVE, rows),
        )


def side_by_side(window_ref, frame, taps, weight):
    return jnp.dot(
        jnp.concatenate([window_ref[frame, slot] for slot, _ in taps], axis=-1),
        jnp.concatenate([weight[tap] for _, tap in taps], axis=0),
        preferred_element_type=F32,
    )


def last_kernel(
    flag_ref, prior_ref, pair_ref, cross_ref, gain1_ref, weight1_ref, gain2_ref,
    weight2_ref, bias2_ref, first_ref, next_ref, late_ref, inner_ref, two_ref, four_ref, odd_ref, out_ref,
    window_ref, stage_ref, strided_ref, total_ref,
):
    first_row, keep, distance = holds(flag_ref, TOP), holds(flag_ref, FULL), flag_ref[DISTANCE : DISTANCE + 1]
    rows, width, channels = prior_ref.shape[1:]
    outer = (0, 1, rows + ABOVE)
    for frame in range(2):
        reader = row_reader(flag_ref, prior_ref, frame, pair_ref, cross_ref)
        fill_hidden(
            lambda slot: reader(outer[slot]), gain1_ref[...], window_ref, frame, range(len(outer))
        )
    for target in (0, 1, rows):
        taps = [(slot, place - target) for slot, place in enumerate(outer) if 0 <= place - target < 3]
        total_ref[0, target] = next_ref[target]
        total_ref[1, target] = first_ref[target]
        both = side_by_side(window_ref, 1, taps, beside(weight1_ref, 0, 1))
        total_ref[0, target] += both[:, :channels]
        total_ref[1, target] += both[:, channels:] + side_by_side(
            window_ref, 0, taps, weight1_ref[0]
        )
    for slot in range(2):
        strided_ref[slot, ABOVE:rows] = inner_ref[slot, ABOVE:rows]
        fill_second(
            lambda row: total_ref[slot, row],
            gain2_ref[...], first_row, stage_ref, strided_ref, slot, (0, 1, rows),
        )
    shape = out_ref.shape[1:]
    half = strided_ref.shape[2]
    late = late_ref[...] + conv2_frame(weight2_ref, (strided_ref, 0, 0))
    out_ref[1] = jnp.where(jnp.concatenate([keep, keep], axis=-1), late, 0.0).astype(BF16).reshape(shape)
    early = conv2_frame(weight2_ref, (strided_ref, 0, 2), (strided_ref, 1, 1))
    for row in range(shape[0]):
        tail = chosen(
            distance, two_ref[row].astype(F32), four_ref[row].astype(F32), odd_ref[row].astype(F32)
        )
        tail = jnp.concatenate([tail[:half], tail[half:]], axis=-1)
        part = early[row * half : (row + 1) * half] + bias2_ref[...]
        out_ref[0, row] = (part + tail).astype(BF16)


def call(kernel, operands, outs, scratch, flops=0):
    moved = sum(o.size * o.dtype.itemsize for o in list(operands) + list(outs))
    return pl.pallas_call(
        kernel,
        out_shape=outs,
        in_specs=[pl.BlockSpec(memory_space=VMEM)] * len(operands),
        out_specs=[pl.BlockSpec(memory_space=VMEM)] * len(outs),
        scratch_shapes=scratch,
        compiler_params=pltpu.CompilerParams(vmem_limit_bytes=14 * 1024 * 1024),
        cost_estimate=pl.CostEstimate(flops=flops, bytes_accessed=moved, transcendentals=0),
    )(*operands)


def per_device(
    video_frames, pred_owner, frame_counts, norm1_gain, conv1_weight, conv1_bias, norm2_gain,
    conv2_weight, conv2_bias,
):
    frames, rows, width, channels = video_frames.shape
    wide = conv2_weight.shape[-1]
    half = width // 2
    position = lax.axis_index("group")
    band = lax.axis_index("row")
    distance = jnp.where(pred_owner[0] >= 0, position - pred_owner[0], 0)
    marks = [
        band % 2 == 0, band == 0, frame_counts[0] >= frames, distance,
        band == lax.axis_size("row") - 1, position % 2 == 0,
    ]
    marks += [0] * (8 - len(marks))
    flags = jnp.stack([jnp.full((channels,), mark, F32) for mark in marks])

    def like(value, dtype=BF16):
        return jax.ShapeDtypeStruct(value, dtype)

    def window(count, high):
        return VMEM((count, high, width, 3 * channels), BF16)

    def for_partner(own, near, far, start=0):
        kernel = functools.partial(partner_kernel, start)
        return call(kernel, [flags, wanted, own, near, far], [like(far.shape)], [])[0]

    weight1 = conv1_weight.reshape(3, 3, 3 * channels, channels)
    weight2 = conv2_weight.reshape(3, 3, 3 * channels, wide)
    gain1, bias1 = norm1_gain[None], conv1_bias[None]
    gain2, bias2 = norm2_gain[None], conv2_bias[None]
    pair_of = like((2, rows, width, channels))
    flat = (2 * rows, width, channels)
    total = (rows + 1, width, channels)
    stage = VMEM((rows + 1, width + 16, channels), F32)
    strided = VMEM((2, rows + 1, half, 3 * channels), BF16)
    one_tap = 2 * (rows + 1) * width * 9 * channels * channels
    one_code = 2 * (rows // 2) * half * 9 * channels * wide

    edge = like((frames, ABOVE, width, channels))
    own, pair, cross = call(
        pack_kernel, [flags, video_frames], [pair_of, edge, edge], [], flops=PACK
    )
    wanted = swapped(jnp.full((8, channels), distance, F32), "group")
    cross = crossed(after(wanted, cross)[0])
    own = own.reshape(flat)
    near = rotated(own, "group", 2)
    pair = swapped(pair, "row")
    fars = [
        relayed(lax.slice_in_dim(near, frame * rows, (frame + 1) * rows, axis=0))
        for frame in range(2)
    ]
    pair, cross = after(near, pair, cross)
    def windows(count):
        return like((count, rows + 3, width, 3 * channels))

    own_e, strided3, later = call(
        send_kernel,
        [flags, video_frames, pair, cross, gain1, weight1, bias1, gain2, weight2],
        [
            like((rows // 2, width, channels)), like((1, rows + 1, half, 3 * channels)),
            windows(3),
        ],
        [stage, VMEM(total, F32)],
        flops=3 * one_tap + one_code,
    )
    chosen_first = for_partner(own, near, after(own_e, fars[0])[0])
    chosen_own = for_partner(own, near, after(chosen_first, fars[1])[0], rows)
    odds = [swapped(chosen_first, "group"), swapped(chosen_own, "group")]
    near_e = after(chosen_own, rotated(own_e, "group", 2))[0]
    far_e = relayed(near_e)
    first, following, start = call(
        own_kernel,
        [
            flags, video_frames, pair, cross, gain1, weight1, bias1, after(near_e, later)[0],
        ],
        [like(total, F32), like(total, F32), windows(1)],
        [],
        flops=WHILE_SWAPPED,
    )
    odd_e = swapped(for_partner(own_e, near_e, far_e), "group")
    edge = like((2, ABOVE, width, channels))
    prior, prior_pair, prior_cross = call(
        prior_kernel, [flags, near] + fars + [odds[0], after(first, odds[1])[0]], [pair_of, edge, edge], []
    )
    (late,) = call(
        second_kernel,
        [
            flags, video_frames, pair, cross, weight1, bias1, gain2, weight2, bias2,
            after(prior, strided3)[0], start, later,
        ],
        [like((rows // 2 * half, wide), F32)],
        [stage, strided, VMEM(total, F32)],
        flops=WHILE_SENT,
    )
    prior_cross = crossed_late(prior_cross)
    prior_pair = swapped(prior_pair, "row")
    first, following, inner = call(
        inner_kernel,
        [flags, prior, gain1, weight1, gain2, first, following],
        [like(total, F32), like(total, F32), like((2, rows + 1, half, 3 * channels))],
        [window(2, rows), stage],
        flops=2 * one_tap,
    )
    return call(
        last_kernel,
        [flags, prior, prior_pair, prior_cross, gain1, weight1, gain2, weight2, bias2, first,
         following, late, inner, near_e, far_e, odd_e],
        [like((frames // 2, rows // 2, half, wide))],
        [window(2, 3), stage, strided, VMEM((2,) + total, F32)],
        flops=one_tap + 3 * one_code,
    )[0]


def solution(mesh):
    placed = (P("group", "row", None, None), P("group"), P("group"), P(), P(), P(), P(), P(), P())
    return jax.shard_map(
        per_device,
        mesh=mesh,
        in_specs=placed,
        out_specs=P("group", "row", None, None),
        check_vma=False,
    )
```

```python
import functools

import jax
import jax.numpy as jnp
from jax import lax
from jax.experimental import pallas as pl
from jax.experimental.pallas import tpu as pltpu
from jax.sharding import PartitionSpec as P

ABOVE = 2
EVEN, TOP, FULL, DISTANCE, BOTTOM, EVEN_GROUP = range(6)
PACK = 30_000_000_000
WHILE_SWAPPED = 3_000_000_000
WHILE_SENT = 200_000_000
VMEM = pltpu.VMEM
F32 = jnp.float32
BF16 = jnp.bfloat16


def rotated(value, axis, steps):
    count = lax.axis_size(axis)
    return lax.ppermute(value, axis, [(source, (source + steps) % count) for source in range(count)])


def relayed(value):
    groups, rows = lax.axis_size("group"), lax.axis_size("row")
    pairs = []
    for group in range(groups):
        for row in range(rows):
            if group < 2:
                target = (group, row ^ 1)
            else:
                target = (group + 2 if group + 2 < groups else group + 4 - groups, row)
            pairs.append((group * rows + row, target[0] * rows + target[1]))
    return lax.ppermute(value, ("group", "row"), pairs)


def swapped(value, axis):
    return lax.ppermute(value, axis, [(place, place ^ 1) for place in range(lax.axis_size(axis))])


def crossed_late(value):
    groups, rows = lax.axis_size("group"), lax.axis_size("row")
    planes = groups // 2
    pairs = []
    for group in range(groups):
        plane = group // 2
        for row in range(rows):
            if 0 < row < rows - 1:
                target = (group, ((row + 1) ^ 1) - 1)
            elif 0 < plane < planes - 1 and planes % 2 == 0:
                target = (2 * (((plane + 1) ^ 1) - 1) + group % 2, row)
            else:
                target = (group, rows - 1 - row)
            pairs.append((group * rows + row, target[0] * rows + target[1]))
    return lax.ppermute(value, ("group", "row"), pairs)


def crossed(value):
    groups, rows = lax.axis_size("group"), lax.axis_size("row")
    pairs = []
    for group in range(groups):
        for row in range(rows):
            outer = row in (0, rows - 1)
            target = (group ^ 1, row) if outer else (group, ((row + 1) ^ 1) - 1)
            pairs.append((group * rows + row, target[0] * rows + target[1]))
    return lax.ppermute(value, ("group", "row"), pairs)


def after(first, *values):
    return lax.optimization_barrier((first,) + values)[1:]


def pixel_silu(values, gain):
    inverse = lax.rsqrt(jnp.mean(values * values, axis=-1, keepdims=True) + 1e-06)
    half = values * inverse * (0.5 * gain)
    return half + half * jnp.tanh(half)


def column_window(row):
    width = row.shape[0]
    column = lax.broadcasted_iota(jnp.int32, row.shape, 0)
    left = jnp.where(column == 0, 0.0, pltpu.roll(row, 1, 0))
    right = jnp.where(column == width - 1, 0.0, pltpu.roll(row, width - 1, 0))
    return jnp.concatenate([left.astype(BF16), row.astype(BF16), right.astype(BF16)], axis=-1)


def holds(flag_ref, index):
    return flag_ref[index : index + 1] != 0


def fill_hidden(read, gain, window_ref, frame, rows):
    for row in rows:
        window_ref[frame, row] = column_window(pixel_silu(read(row), gain))


def conv1_rows(window_ref, frame, rows, weight):
    width, depth = window_ref.shape[2], window_ref.shape[3]
    window = jnp.concatenate(
        [window_ref[frame, tap : tap + rows].reshape(rows * width, depth) for tap in range(3)],
        axis=-1,
    )
    return jnp.dot(window, weight.reshape(3 * depth, weight.shape[2]), preferred_element_type=F32)


def fill_second(values, gain, first_row, stage_ref, strided_ref, slot, rows):
    half = strided_ref.shape[2]
    width, channels = 2 * half, stage_ref.shape[2]
    for row in rows:
        ready = pixel_silu(values(row), gain).astype(BF16).astype(F32)
        if row == 0:
            ready = jnp.where(first_row, 0.0, ready)
        stage_ref[row, 0:8] = jnp.zeros((8, channels), F32)
        stage_ref[row, 8 : 8 + width] = ready
        strided_ref[slot, row] = jnp.concatenate(
            [stage_ref[row, pl.ds(7 + tap, half, stride=2), :].astype(BF16) for tap in range(3)],
            axis=-1,
        )


def conv2_frame(weight_ref, *parts):
    windows, weights = [], []
    for strided_ref, slot, step in parts:
        for tap in range(3):
            windows.append(
                jnp.concatenate([strided_ref[slot, tap], strided_ref[slot, tap + 2]], axis=0)
            )
            weights.append(weight_ref[step, tap])
    return jnp.dot(
        jnp.concatenate(windows, axis=-1), jnp.concatenate(weights, axis=0), preferred_element_type=F32
    )


def row_reader(flag_ref, video_ref, frame, pair_ref, cross_ref):
    even, top, bottom = holds(flag_ref, EVEN), holds(flag_ref, TOP), holds(flag_ref, BOTTOM)
    rows = video_ref.shape[1]

    def read(row):
        if ABOVE <= row < ABOVE + rows:
            return video_ref[frame, row - ABOVE].astype(F32)
        if row < ABOVE:
            first, second, outside = cross_ref[frame, row], pair_ref[frame, row], top
        else:
            first, second, outside = pair_ref[frame, 0], cross_ref[frame, 0], bottom
        value = jnp.where(even, first.astype(F32), second.astype(F32))
        return jnp.where(outside, 0.0, value)

    return read


def pack_kernel(flag_ref, video_ref, own0_ref, own1_ref, pair_ref, cross_ref):
    even = holds(flag_ref, EVEN)
    frames, rows = video_ref.shape[:2]
    own0_ref[...] = video_ref[frames - 2]
    own1_ref[...] = video_ref[frames - 1]
    split_edges(even, video_ref, frames, rows, pair_ref, cross_ref)


def split_edges(even, source_ref, frames, rows, pair_ref, cross_ref):
    for frame in range(frames):
        for row in range(ABOVE):
            high, low = source_ref[frame, row], source_ref[frame, rows - ABOVE + row]
            pair_ref[frame, row] = jnp.where(even, low, high)
            cross_ref[frame, row] = jnp.where(even, high, low)


def beside(weight_ref, *steps):
    return jnp.concatenate([weight_ref[step] for step in steps], axis=-1)


def send_kernel(
    flag_ref, video_ref, pair_ref, cross_ref, gain1_ref, weight1_ref, bias1_ref,
    gain2_ref, weight2_ref, tail_ref, strided_out_ref, window_ref, stage_ref, total_ref,
):
    first_row = holds(flag_ref, TOP)
    channels = video_ref.shape[3]
    readers = [row_reader(flag_ref, video_ref, f, pair_ref, cross_ref) for f in range(4)]
    for slot, frame in enumerate((1, 2, 3)):
        fill_hidden(readers[frame], gain1_ref[...], window_ref, slot, range(7))
    total_ref[...] = sum(
        conv1_rows(window_ref, step, 5, weight1_ref[step]) for step in range(3)
    ).reshape(total_ref.shape)
    fill_second(
        lambda row: total_ref[row] + readers[3](row + 1) + bias1_ref[...],
        gain2_ref[...], first_row, stage_ref, strided_out_ref, 0, range(5),
    )
    tail = conv2_frame(weight2_ref, (strided_out_ref, 0, 0)).astype(BF16)
    half = strided_out_ref.shape[2]
    for row in range(tail_ref.shape[0]):
        for part in range(2):
            tail_ref[row, part * half : (part + 1) * half] = tail[
                row * half : (row + 1) * half, part * channels : (part + 1) * channels
            ]


def second_kernel(
    flag_ref, video_ref, pair_ref, cross_ref, gain1_ref, weight1_ref, bias1_ref,
    gain2_ref, weight2_ref, bias2_ref, strided3_ref, later_ref, late_ref, window_ref,
    stage_ref, strided_ref, total_ref,
):
    first_row = holds(flag_ref, TOP)
    readers = [row_reader(flag_ref, video_ref, f, pair_ref, cross_ref) for f in range(4)]
    fill_hidden(readers[0], gain1_ref[...], window_ref, 0, range(7))
    total_ref[...] = (
        conv1_rows(window_ref, 0, 5, weight1_ref[0])
        + conv1_rows(later_ref, 0, 5, weight1_ref[1])
        + conv1_rows(later_ref, 1, 5, weight1_ref[2])
    ).reshape(total_ref.shape)
    fill_second(
        lambda row: total_ref[row] + readers[2](row + 1) + bias1_ref[...],
        gain2_ref[...], first_row, stage_ref, strided_ref, 0, range(5),
    )
    late_ref[...] = (
        conv2_frame(weight2_ref, (strided_ref, 0, 1), (strided3_ref, 0, 2)) + bias2_ref[...]
    )


def own_kernel(
    flag_ref, video_ref, pair_ref, cross_ref, weight1_ref, bias1_ref, window_ref, later_ref,
    first_ref, next_ref,
):
    channels = video_ref.shape[3]
    readers = [row_reader(flag_ref, video_ref, f, pair_ref, cross_ref) for f in range(2)]
    both = conv1_rows(window_ref, 0, 5, beside(weight1_ref, 2, 1))
    first_ref[...] = both[:, :channels].reshape(first_ref.shape)
    next_ref[...] = (
        both[:, channels:] + conv1_rows(later_ref, 0, 5, weight1_ref[2])
    ).reshape(next_ref.shape)
    for row in range(5):
        next_ref[row] += readers[1](row + 1) + bias1_ref[...]
        first_ref[row] += readers[0](row + 1) + bias1_ref[...]


def chosen(distance, two, four, odd):
    value = jnp.where(distance == 2, two, odd)
    value = jnp.where(distance == 4, four, value)
    return jnp.where(distance == 0, 0.0, value)


def partner_kernel(start, flag_ref, wanted_ref, own_ref, near_ref, far_ref, out_ref):
    first, one = holds(flag_ref, EVEN_GROUP), wanted_ref[0:1] == 1
    for row in range(out_ref.shape[0]):
        own, near, far = own_ref[start + row], near_ref[start + row], far_ref[row]
        out_ref[row] = jnp.where(
            first, jnp.where(one, own, near), jnp.where(one, near, far)
        )


def prior_kernel(
    flag_ref, two0_ref, two1_ref, four0_ref, four1_ref, odd0_ref, odd1_ref, prior_ref, pair_ref, cross_ref,
):
    even, distance = holds(flag_ref, EVEN), flag_ref[DISTANCE : DISTANCE + 1]
    frames, rows = prior_ref.shape[:2]
    sources = ((two0_ref, four0_ref, odd0_ref), (two1_ref, four1_ref, odd1_ref))
    for frame, (two_ref, four_ref, odd_ref) in enumerate(sources):
        for row in range(rows):
            prior_ref[frame, row] = chosen(
                distance, two_ref[row], four_ref[row], odd_ref[row]
            )
    split_edges(even, prior_ref, frames, rows, pair_ref, cross_ref)


def inner_kernel(
    flag_ref, prior_ref, gain1_ref, weight1_ref, gain2_ref, first_ref, next_ref,
    first_out_ref, next_out_ref, strided_out_ref, window_ref, stage_ref,
):
    del flag_ref
    rows, width, channels = prior_ref.shape[1:]
    for frame in range(2):
        fill_hidden(
            lambda row: prior_ref[frame, row].astype(F32), gain1_ref[...], window_ref, frame, range(rows)
        )
    first_out_ref[...] = first_ref[...]
    next_out_ref[...] = next_ref[...]
    for tap in range(3):
        low = max(0, ABOVE - tap)
        count = min(rows + 1, rows + ABOVE - tap) - low
        start = low + tap - ABOVE
        shape = (count, width, channels)

        def part(frame, weight):
            window = window_ref[frame, start : start + count]
            return jnp.dot(
                window.reshape(count * width, window.shape[2]), weight, preferred_element_type=F32
            )

        both = part(1, beside(weight1_ref.at[:, tap], 0, 1))
        next_out_ref[low : low + count] += both[:, :channels].reshape(shape)
        first_out_ref[low : low + count] += (
            both[:, channels:] + part(0, weight1_ref[0, tap])
        ).reshape(shape)
    for slot, total_ref in enumerate((next_out_ref, first_out_ref)):
        fill_second(
            lambda row: total_ref[row],
            gain2_ref[...], None, stage_ref, strided_out_ref, slot, range(ABOVE, rows),
        )


def side_by_side(window_ref, frame, taps, weight):
    return jnp.dot(
        jnp.concatenate([window_ref[frame, slot] for slot, _ in taps], axis=-1),
        jnp.concatenate([weight[tap] for _, tap in taps], axis=0),
        preferred_element_type=F32,
    )


def last_kernel(
    flag_ref, prior_ref, pair_ref, cross_ref, gain1_ref, weight1_ref, gain2_ref,
    weight2_ref, bias2_ref, first_ref, next_ref, late_ref, inner_ref, two_ref, four_ref, odd_ref, out_ref,
    window_ref, stage_ref, strided_ref, total_ref,
):
    first_row, keep, distance = holds(flag_ref, TOP), holds(flag_ref, FULL), flag_ref[DISTANCE : DISTANCE + 1]
    rows, width, channels = prior_ref.shape[1:]
    outer = (0, 1, rows + ABOVE)
    for frame in range(2):
        reader = row_reader(flag_ref, prior_ref, frame, pair_ref, cross_ref)
        fill_hidden(
            lambda slot: reader(outer[slot]), gain1_ref[...], window_ref, frame, range(len(outer))
        )
    for target in (0, 1, rows):
        taps = [(slot, place - target) for slot, place in enumerate(outer) if 0 <= place - target < 3]
        total_ref[0, target] = next_ref[target]
        total_ref[1, target] = first_ref[target]
        both = side_by_side(window_ref, 1, taps, beside(weight1_ref, 0, 1))
        total_ref[0, target] += both[:, :channels]
        total_ref[1, target] += both[:, channels:] + side_by_side(
            window_ref, 0, taps, weight1_ref[0]
        )
    for slot in range(2):
        strided_ref[slot, ABOVE:rows] = inner_ref[slot, ABOVE:rows]
        fill_second(
            lambda row: total_ref[slot, row],
            gain2_ref[...], first_row, stage_ref, strided_ref, slot, (0, 1, rows),
        )
    shape = out_ref.shape[1:]
    half = strided_ref.shape[2]
    late = late_ref[...] + conv2_frame(weight2_ref, (strided_ref, 0, 0))
    out_ref[1] = jnp.where(jnp.concatenate([keep, keep], axis=-1), late, 0.0).astype(BF16).reshape(shape)
    early = conv2_frame(weight2_ref, (strided_ref, 0, 2), (strided_ref, 1, 1))
    for row in range(shape[0]):
        tail = chosen(
            distance, two_ref[row].astype(F32), four_ref[row].astype(F32), odd_ref[row].astype(F32)
        )
        tail = jnp.concatenate([tail[:half], tail[half:]], axis=-1)
        part = early[row * half : (row + 1) * half] + bias2_ref[...]
        out_ref[0, row] = (part + tail).astype(BF16)


def call(kernel, operands, outs, scratch, flops=0):
    moved = sum(o.size * o.dtype.itemsize for o in list(operands) + list(outs))
    return pl.pallas_call(
        kernel,
        out_shape=outs,
        in_specs=[pl.BlockSpec(memory_space=VMEM)] * len(operands),
        out_specs=[pl.BlockSpec(memory_space=VMEM)] * len(outs),
        scratch_shapes=scratch,
        compiler_params=pltpu.CompilerParams(vmem_limit_bytes=14 * 1024 * 1024),
        cost_estimate=pl.CostEstimate(flops=flops, bytes_accessed=moved, transcendentals=0),
    )(*operands)


def per_device(
    video_frames, pred_owner, frame_counts, norm1_gain, conv1_weight, conv1_bias, norm2_gain,
    conv2_weight, conv2_bias,
):
    frames, rows, width, channels = video_frames.shape
    wide = conv2_weight.shape[-1]
    half = width // 2
    position = lax.axis_index("group")
    band = lax.axis_index("row")
    distance = jnp.where(pred_owner[0] >= 0, position - pred_owner[0], 0)
    marks = [
        band % 2 == 0, band == 0, frame_counts[0] >= frames, distance,
        band == lax.axis_size("row") - 1, position % 2 == 0,
    ]
    marks += [0] * (8 - len(marks))
    flags = jnp.stack([jnp.full((channels,), mark, F32) for mark in marks])

    def like(value, dtype=BF16):
        return jax.ShapeDtypeStruct(value, dtype)

    def window(count, high):
        return VMEM((count, high, width, 3 * channels), BF16)

    def for_partner(own, near, far, start=0):
        kernel = functools.partial(partner_kernel, start)
        return call(kernel, [flags, wanted, own, near, far], [like(far.shape)], [])[0]

    weight1 = conv1_weight.reshape(3, 3, 3 * channels, channels)
    weight2 = conv2_weight.reshape(3, 3, 3 * channels, wide)
    gain1, bias1 = norm1_gain[None], conv1_bias[None]
    gain2, bias2 = norm2_gain[None], conv2_bias[None]
    pair_of = like((2, rows, width, channels))
    frame_of = like((rows, width, channels))
    total = (rows + 1, width, channels)
    stage = VMEM((rows + 1, width + 16, channels), F32)
    strided = VMEM((2, rows + 1, half, 3 * channels), BF16)
    one_tap = 2 * (rows + 1) * width * 9 * channels * channels
    one_code = 2 * (rows // 2) * half * 9 * channels * wide

    edge = like((frames, ABOVE, width, channels))
    own0, own1, pair, cross = call(
        pack_kernel, [flags, video_frames], [frame_of, frame_of, edge, edge], [], flops=PACK
    )
    wanted = swapped(jnp.full((8, channels), distance, F32), "group")
    cross = crossed(cross)
    nears = [rotated(own0, "group", 2), rotated(own1, "group", 2)]
    pair = swapped(pair, "row")
    fars = [relayed(near) for near in nears]
    pair, cross = after(nears[1], pair, cross)
    def windows(count):
        return like((count, rows + 3, width, 3 * channels))

    own_e, strided3, later = call(
        send_kernel,
        [flags, video_frames, pair, cross, gain1, weight1, bias1, gain2, weight2],
        [
            like((rows // 2, width, channels)), like((1, rows + 1, half, 3 * channels)),
            windows(3),
        ],
        [stage, VMEM(total, F32)],
        flops=3 * one_tap + one_code,
    )
    chosen_first = for_partner(own0, nears[0], after(own_e, fars[0])[0])
    chosen_own = for_partner(own1, nears[1], after(chosen_first, fars[1])[0])
    odds = [swapped(chosen_first, "group"), swapped(chosen_own, "group")]
    near_e = after(chosen_own, rotated(own_e, "group", 2))[0]
    late, start = call(
        second_kernel,
        [
            flags, video_frames, pair, cross, gain1, weight1, bias1, gain2, weight2, bias2,
            after(near_e, strided3)[0], later,
        ],
        [like((rows // 2 * half, wide), F32), windows(1)],
        [stage, strided, VMEM(total, F32)],
        flops=WHILE_SWAPPED,
    )
    far_e = relayed(near_e)
    first, following = call(
        own_kernel,
        [flags, video_frames, pair, cross, weight1, bias1, start, later],
        [like(total, F32), like(total, F32)],
        [],
        flops=WHILE_SENT,
    )
    odd_e = swapped(for_partner(own_e, near_e, far_e), "group")
    edge = like((2, ABOVE, width, channels))
    prior, prior_pair, prior_cross = call(
        prior_kernel, [flags] + nears + fars + [odds[0], after(late, odds[1])[0]], [pair_of, edge, edge], []
    )
    prior_cross = crossed_late(prior_cross)
    prior_pair = swapped(prior_pair, "row")
    first, following, inner = call(
        inner_kernel,
        [flags, prior, gain1, weight1, gain2, first, following],
        [like(total, F32), like(total, F32), like((2, rows + 1, half, 3 * channels))],
        [window(2, rows), stage],
        flops=2 * one_tap,
    )
    return call(
        last_kernel,
        [flags, prior, prior_pair, prior_cross, gain1, weight1, gain2, weight2, bias2, first,
         following, late, inner, near_e, far_e, odd_e],
        [like((frames // 2, rows // 2, half, wide))],
        [window(2, 3), stage, strided, VMEM((2,) + total, F32)],
        flops=one_tap + 3 * one_code,
    )[0]


def solution(mesh):
    placed = (P("group", "row", None, None), P("group"), P("group"), P(), P(), P(), P(), P(), P())
    return jax.shard_map(
        per_device,
        mesh=mesh,
        in_specs=placed,
        out_specs=P("group", "row", None, None),
        check_vma=False,
    )
```
